256 devices in a mesh: tile: 64 (over z, y, core), freq: 4 (over x).
Axes of the slice: x: 4, y: 4, z: 8, core: 2. Of those that a mesh axis runs over, the one named last changes fastest.
Arguments:
- displacement: float32 [2, 3, 512, 48, 256], P(None, None, ('freq', 'tile')), parts along dimension 2, may hold values from -6 to 6
- cell_scale: float32 [128, 48, 256], P('tile'), may hold values from 0.5 to 2
- material_id: int32 [128, 48, 256], P('tile'), may hold values from 0 to 15
- stiff_table: float32 [2, 64], P(None, 'freq'), parts along dimension 1, may hold values from 0.2 to 1.5
- mass_table: float32 [2, 64], P(None, 'freq'), parts along dimension 1, may hold values from -1 to 0.5
- pile_block: bfloat16 [256, 2, 1152, 1152], P(('freq', 'tile')), parts along dimension 0, may hold values from -0.125 to 0.125
- pile_owner: int32 [256], P('freq'), parts along dimension 0, may hold values from 0 to 63, each once
- node_index: int32 [64, 3, 128], replicated, may hold values from 0 to 1572863, as said below
Outputs:
- result: float32 [2, 3, 512, 48, 256], P(None, None, ('freq', 'tile')), parts along dimension 2
The draws below stay inside these ranges and needn't reach their ends.
There are 4 independent parts, one for each index of `freq`. The reference program is written for one: setup_inputs(seed, part) draws one part's arguments, and reference() takes and returns one part's arrays. A program takes and returns all parts, laid end to end along the dimension named above; an argument that names none is the same for every part. Nothing has to cross between parts.
Inputs may be any that keep to these rules, and one draw needn't show every extreme that they name: `node_index`: each pile stands at one position along the farm: its blocks of 128 nodes lie in the cells of one tile of 2 planes, its lower blocks on some piles in the next tile; no cell appears twice; a tile holds at most 8 blocks, and some tile exactly 8.
All inputs are finite; a program needn't handle non-finite values.
Results may differ from the reference program's by a relative error of at most 0.0003.
Values may be sent and summed in bfloat16 or wider, within the bound.
No kernel may reach another device: no remote copies, remote signals or barrier semaphores. Data moves between devices by JAX's collectives and lax.ppermute only.
A program may use at most 64 MiB of HBM per device.

```python
import math
import jax
import jax.numpy as jnp
from jax import lax

CX = 2
NY = 48
NZ = 256
ORDER = 1152
BLOCK_ROWS = 128
MOST = 8
NLAYER = 8
ABS = 3
NB = 3
PILES = 64
NX = 128
NMAT = 16


def draw_material_id(key, part):
    jitter = jax.random.randint(key, (NLAYER - 1,), -2, 3)
    bounds = jnp.arange(1, NLAYER) * NZ // NLAYER + jitter
    depth = jnp.arange(NZ)
    layer = jnp.sum((depth[None, :] >= bounds[:, None]).astype(jnp.int32), axis=0)
    along = jnp.arange(NX)
    across = jnp.arange(NY)
    edge_along = (along < ABS) | (along >= NX - ABS)
    edge_across = (across < ABS) | (across >= NY - ABS)
    bottom = depth >= NZ - ABS
    sponge = edge_along[:, None, None] | edge_across[None, :, None] | bottom[None, None, :]
    return (layer[None, None, :] + NLAYER * sponge.astype(jnp.int32)).astype(jnp.int32)


def draw_node_index(key, part):
    key_place = jax.random.fold_in(key, 21)
    key_split = jax.random.fold_in(key, 22)
    key_busy = jax.random.fold_in(key, 23)
    key_cells = jax.random.fold_in(key, 24)
    pile_range = jnp.arange(PILES, dtype=jnp.int32)
    placed = jax.random.permutation(key_place, PILES).astype(jnp.int32)
    kept = jax.random.randint(key_split, (PILES,), 1, NB + 1).astype(jnp.int32)
    busy = jax.random.randint(key_busy, (), 1, PILES - 1).astype(jnp.int32)
    standing = jnp.zeros((PILES,), jnp.int32).at[placed].set(pile_range)
    pile_here = standing[busy]
    pile_next = standing[busy + 1]
    pile_before = standing[busy - 1]
    base_tile = jnp.where(pile_range == pile_next, busy, placed)
    kept = jnp.where((pile_range == pile_here) | (pile_range == pile_next), NB, kept)
    kept = jnp.where(pile_range == pile_before, 1, kept)
    kept = jnp.where(base_tile == PILES - 1, NB, kept)
    block_range = jnp.arange(NB, dtype=jnp.int32)
    lower = (block_range[None, :] >= kept[:, None]).astype(jnp.int32)
    tile_of = (base_tile[:, None] + lower).reshape(-1)
    flat_range = jnp.arange(PILES * NB, dtype=jnp.int32)
    earlier = (tile_of[:, None] == tile_of[None, :]) & (flat_range[None, :] < flat_range[:, None])
    slot_of = jnp.sum(earlier.astype(jnp.int32), axis=1)
    cell_total = CX * NY * NZ
    tile_cells = jax.vmap(lambda sub_key: jax.random.permutation(sub_key, cell_total)[:MOST * BLOCK_ROWS])(jax.random.split(key_cells, PILES))
    tile_cells = tile_cells.reshape(PILES, MOST, BLOCK_ROWS)
    local_cells = tile_cells[tile_of, slot_of]
    global_cells = tile_of[:, None] * cell_total + local_cells
    return global_cells.reshape(PILES, NB, BLOCK_ROWS).astype(jnp.int32)


def shard_levels(stream_key, shape, pieces, smallest, high):
    level = 1.0
    for axis_at, shards_of in pieces:
        steps = jax.random.uniform(jax.random.fold_in(jax.random.fold_in(stream_key, 6), axis_at), (shards_of,), jnp.float32, smallest / len(pieces), high / len(pieces))
        level = level * jnp.repeat(jnp.exp(steps), shape[axis_at] // shards_of).reshape((-1,) + (1,) * (len(shape) - 1 - axis_at))
    return level


def gaussian(own_key, shape, scale, limit, shards=(), kind=jnp.bfloat16):
    loudness = shard_levels(own_key, shape, shards, -0.22, 0.18) if shards else 1.0
    array = jax.random.normal(own_key, shape, jnp.float32) * scale * loudness
    return jnp.minimum(jnp.maximum(array, -limit), limit).astype(kind)


def setup_inputs(seed: int = 0, part: int = 0) -> dict:
    arg_keys = jax.random.split(jax.random.key(seed), 9)
    part_keys = jax.random.split(jax.random.fold_in(arg_keys[8], part), 9)
    return {
        "displacement": gaussian(part_keys[0], (2, 3, NX, NY, NZ), 1.0, 6.0, ((2, 64),), jnp.float32),
        "cell_scale": jnp.clip(jnp.exp(math.log(2.0) - 1.3862944 * jax.random.uniform(arg_keys[1], (NX, NY, NZ), jnp.float32) ** shard_levels(arg_keys[1], (NX, NY, NZ), ((0, 64),), -0.2, 0.2)), 0.5, 2.0),
        "material_id": draw_material_id(jax.random.fold_in(arg_keys[8], 71), part),
        "stiff_table": jnp.clip(jax.random.uniform(part_keys[3], (2, NMAT), jnp.float32, 0.2, 1.5), 0.2, 1.5),
        "mass_table": jnp.clip(jax.random.uniform(part_keys[4], (2, NMAT), jnp.float32, -1.0, 0.5), -1.0, 0.5),
        "pile_block": gaussian(part_keys[5], (PILES, 2, ORDER, ORDER), (2 * ORDER) ** -0.5, 0.125, ((0, 64),)),
        "pile_owner": jax.random.permutation(part_keys[6], PILES).astype(jnp.int32),
        "node_index": draw_node_index(jax.random.fold_in(arg_keys[8], 71), part),
    }


def soil_apply(padded, inertia):
    centre = padded[:, 1:-1, 1:-1, 1:-1]
    extent = centre.shape[1:]
    displace = centre[:6].reshape((2, 3) + extent)
    stiffness = centre[6:]
    total_real = inertia[0] * displace[0] - inertia[1] * displace[1]
    total_imag = inertia[0] * displace[1] + inertia[1] * displace[0]
    for direction in range(3):
        for offset in (0, 2):
            window = [slice(None), slice(1, -1), slice(1, -1), slice(1, -1)]
            window[direction + 1] = slice(offset, offset + extent[direction])
            beside = padded[tuple(window)]
            face_real = 0.5 * (stiffness[0] + beside[6])
            face_imag = 0.5 * (stiffness[1] + beside[7])
            strain = displace - beside[:6].reshape(displace.shape)
            total_real = total_real + face_real * strain[0] - face_imag * strain[1]
            total_imag = total_imag + face_real * strain[1] + face_imag * strain[0]
    return jnp.stack([total_real, total_imag])


def reference(displacement, cell_scale, material_id, stiff_table, mass_table, pile_block, pile_owner, node_index):
    extent = cell_scale.shape
    stiffness = stiff_table[:, material_id] * cell_scale
    inertia = mass_table[:, material_id]
    stacked = jnp.concatenate([displacement.reshape((6,) + extent), stiffness], axis=0)
    padded = jnp.pad(stacked, ((0, 0), (1, 1), (1, 1), (1, 1)))
    soil_term = soil_apply(padded, inertia)
    flat_nodes = node_index.reshape(-1)
    pile_count = node_index.shape[0]
    gathered = displacement.reshape(6, -1)[:, flat_nodes]
    interface = gathered.reshape(2, 3, pile_count, NB, BLOCK_ROWS).transpose(2, 0, 1, 3, 4)
    interface = interface.reshape(pile_count, 2, ORDER).astype(jnp.bfloat16)

    def apply_pile(inputs):
        vector, slot_index = inputs
        matrix = pile_block[slot_index]
        real_part = jnp.dot(matrix[0], vector[0], preferred_element_type=jnp.float32) - jnp.dot(matrix[1], vector[1], preferred_element_type=jnp.float32)
        imag_part = jnp.dot(matrix[0], vector[1], preferred_element_type=jnp.float32) + jnp.dot(matrix[1], vector[0], preferred_element_type=jnp.float32)
        return jnp.stack([real_part, imag_part]).astype(jnp.bfloat16)

    traction = lax.map(apply_pile, (interface, pile_owner))
    spread = traction.astype(jnp.float32).reshape(pile_count, 2, 3, NB, BLOCK_ROWS).transpose(1, 2, 0, 3, 4).reshape(6, -1)
    result = soil_term.reshape(6, -1).at[:, flat_nodes].add(spread)
    return result.reshape(soil_term.shape)
```

```python
import functools

import jax
import jax.numpy as jnp
from jax import lax
from jax.experimental import pallas as pl
from jax.experimental.pallas import tpu as pltpu
from jax.sharding import PartitionSpec as P

MOST = 8
F32 = jnp.float32
BF16 = jnp.bfloat16
I32 = jnp.int32
NT = (((1,), (1,)), ((), ()))


def iota(shape, axis):
    return lax.broadcasted_iota(I32, shape, axis)


def onehot(mask):
    return jnp.where(mask, 1.0, 0.0).astype(BF16)


def dot(left, right):
    return jnp.dot(left, right, preferred_element_type=F32)


def dot_nt(left, right):
    return lax.dot_general(left, right, NT, preferred_element_type=F32)


def slots_of(nodes, me, cells, columns):
    blocks, width = nodes.shape
    local = nodes - me * cells
    inside = (local >= 0) & (local < cells)
    shift = columns.bit_length() - 1
    row1 = jnp.where(inside, (local >> shift) + 1, 0).astype(F32).astype(BF16)
    column = jnp.where(inside, local & (columns - 1), 0).astype(F32).astype(BF16)
    first = onehot(iota((MOST, width), 1) == 0)
    onto = dot_nt(first, onehot(inside))
    upper = onehot(iota((blocks, blocks), 0) < iota((blocks, blocks), 1))
    rank = dot(onto.astype(BF16), upper)
    slot = onehot((onto > 0.5) & (rank == iota((MOST, blocks), 0).astype(F32)))
    slot_row = dot(slot, row1).astype(I32) - 1
    slot_column = dot(slot, column).astype(I32)
    return slot, slot_row, slot_column


def target_row(owner_ref, tiles):
    owner = owner_ref[...]
    return jnp.concatenate([owner + (b * tiles + 1) for b in range(3)], axis=1)


def gather_kernel(tiles, displacement_ref, nodes_ref, owner_ref, payload_ref, row_ref, column_ref, info_ref, picked):
    me = lax.axis_index("tile")
    components, rows, columns = displacement_ref.shape
    blocks, width = nodes_ref.shape
    block_count = blocks // tiles
    nodes = nodes_ref[...]
    cells = rows * columns
    slot, slot_row, slot_column = slots_of(nodes, me, cells, columns)
    row_ref[...] = slot_row
    column_ref[...] = slot_column
    target = jnp.broadcast_to(target_row(owner_ref, tiles), (MOST, blocks))
    slot_target = dot_nt(target.astype(F32).astype(BF16), slot).astype(I32) - 1
    place = onehot(iota((blocks, MOST), 0) == slot_target[0:1, :])
    field = displacement_ref[...].reshape(components * rows, columns).astype(BF16)
    for s in range(MOST):
        at_column = onehot(iota((columns, width), 0) == slot_column[s : s + 1, :])
        taken = dot(field, at_column)
        at_row = iota((rows, width), 0) == slot_row[s : s + 1, :]
        for c in range(components):
            one = jnp.where(at_row, taken[c * rows : (c + 1) * rows], 0.0)
            picked[s : s + 1, c * width : (c + 1) * width] = jnp.sum(one, axis=0, keepdims=True)
    sent = dot(place, picked[...].astype(BF16)).astype(BF16)
    for b in range(block_count):
        for c in range(components):
            start = (c * block_count + b) * width
            payload_ref[:, start : start + width] = sent[b * tiles : (b + 1) * tiles, c * width : (c + 1) * width]
    owner = owner_ref[...]
    mine = jnp.where(owner == me, 1.0, 0.0)
    first = onehot(iota((MOST, width), 1) == 0)
    tile_of = jnp.floor(((nodes >> 13).astype(F32) + 0.5) * (1.0 / (cells >> 13)))
    tile_row = dot_nt(first, tile_of.astype(BF16))[0:1, :]
    for b in range(block_count):
        info_ref[b : b + 1, :] = jnp.broadcast_to(
            jnp.sum(tile_row[:, b * tiles : (b + 1) * tiles] * mine, axis=1, keepdims=True).astype(I32),
            (1, info_ref.shape[1]),
        )
    target_column = jnp.sum(
        jnp.where(iota((MOST, MOST), 0) == iota((MOST, MOST), 1), slot_target, 0), axis=1, keepdims=True
    )
    info_ref[MOST : 2 * MOST, :] = jnp.broadcast_to(target_column, (MOST, info_ref.shape[1]))


def pile_kernel(arrived_ref, block_ref, info_ref, payload_ref):
    tiles = payload_ref.shape[0]
    order = block_ref.shape[1]
    width = info_ref.shape[1]
    vector = jnp.sum(arrived_ref[...].astype(F32), axis=0).astype(BF16)
    by_real = dot_nt(vector, block_ref[0])
    by_imag = dot_nt(vector, block_ref[1])
    real = by_real[0:1] - by_imag[1:2]
    imag = by_real[1:2] + by_imag[0:1]
    device = iota((tiles, width), 0)
    for i, part in enumerate((real, imag)):
        for k in range(order // width):
            b = k % 3
            piece = jnp.where(device == info_ref[b : b + 1, :], part[:, k * width : (k + 1) * width], 0.0)
            start = i * order + k * width
            payload_ref[:, start : start + width] = piece.astype(BF16)


def scatter_kernel(tiles, soil_ref, arrived_ref, row_ref, column_ref, info_ref, result_ref, spread):
    components, rows, columns = soil_ref.shape
    width = row_ref.shape[1]
    for s in range(MOST):
        target = info_ref[MOST + s, 0]
        target = jnp.maximum(target, 0)
        b = target // tiles
        source = target - b * tiles
        at_row = iota((rows, width), 0) == row_ref[s : s + 1, :]
        for c in range(components // 2):
            piece = arrived_ref[source, :, pl.ds(pl.multiple_of((c * 3 + b) * width, width), width)].astype(F32)
            for i in range(2):
                k = i * (components // 2) + c
                spread[k * rows : (k + 1) * rows, s * width : (s + 1) * width] = jnp.where(
                    at_row, piece[i : i + 1, :], 0.0
                ).astype(BF16)
    at_column = jnp.concatenate(
        [onehot(iota((columns, width), 0) == column_ref[s : s + 1, :]) for s in range(MOST)], axis=1
    )
    added = dot_nt(spread[...], at_column)
    result_ref[...] = soil_ref[...] + added.reshape(components, rows, columns)


def lookup(table_ref, row, kind):
    bits = [(kind & (1 << k)) != 0 for k in range(4)]
    level = [table_ref[row, k] for k in range(16)]
    for bit in bits:
        level = [jnp.where(bit, level[2 * k + 1], level[2 * k]) for k in range(len(level) // 2)]
    return level[0]


def soil_kernel(displacement_ref, scale_ref, kind_ref, before_ref, after_ref, stiff_ref, mass_ref, soil_ref):
    _, planes, ny, nz = displacement_ref.shape
    shape = (ny, nz)
    at_y, at_z = iota(shape, 0), iota(shape, 1)
    y_last, z_last = at_y == ny - 1, at_z == nz - 1
    edges = (
        jnp.where(at_y == 0, 0.5, 0.0)
        + jnp.where(y_last, 0.5, 0.0)
        + jnp.where(at_z == 0, 0.5, 0.0)
        + jnp.where(z_last, 0.5, 0.0)
    )

    def half_stiffness(kind, scale):
        return [0.5 * (lookup(stiff_ref, i, kind) * scale) for i in range(2)]

    def field(x):
        if x < 0:
            return [before_ref[k] for k in range(6)]
        if x >= planes:
            return [after_ref[k] for k in range(6)]
        return [displacement_ref[k, x] for k in range(6)]

    half = [half_stiffness(before_ref[7].astype(I32), before_ref[6])]
    half += [half_stiffness(kind_ref[x], scale_ref[x]) for x in range(planes)]
    half += [half_stiffness(after_ref[7].astype(I32), after_ref[6])]

    def flux(face, near, far):
        strain = [near[k] - far[k] for k in range(6)]
        real = [face[0] * strain[c] - face[1] * strain[3 + c] for c in range(3)]
        imag = [face[0] * strain[3 + c] + face[1] * strain[c] for c in range(3)]
        return real + imag

    def x_flux(x):
        face = [half[x + 1][i] + half[x + 2][i] for i in range(2)]
        return flux(face, field(x), field(x + 1))

    flux_before = x_flux(-1)
    for x in range(planes):
        u = field(x)
        own = half[x + 1]
        diagonal = [lookup(mass_ref, i, kind_ref[x]) + 2.0 * edges * own[i] for i in range(2)]
        total = [diagonal[0] * u[c] - diagonal[1] * u[3 + c] for c in range(3)]
        total += [diagonal[0] * u[3 + c] + diagonal[1] * u[c] for c in range(3)]
        flux_after = x_flux(x)
        total = [total[k] + flux_after[k] - flux_before[k] for k in range(6)]
        flux_before = flux_after
        for axis, last in ((0, y_last), (1, z_last)):
            size = shape[axis]
            face = [jnp.where(last, 0.0, own[i] + pltpu.roll(own[i], size - 1, axis)) for i in range(2)]
            beside = [pltpu.roll(u[k], size - 1, axis) for k in range(6)]
            along = flux(face, u, beside)
            total = [total[k] + along[k] - pltpu.roll(along[k], 1, axis) for k in range(6)]
        for k in range(6):
            soil_ref[k, x] = total[k]


def halos(displacement, cell_scale, kind):
    size = lax.axis_size("tile")
    up = [(i, i + 1) for i in range(size - 1)]
    down = [(j, i) for i, j in up]

    def plane(x):
        return jnp.concatenate([displacement[:, x], cell_scale[x][None], kind[x][None].astype(F32)], axis=0)

    before = lax.ppermute(plane(displacement.shape[1] - 1), "tile", up)
    after = lax.ppermute(plane(0), "tile", down)
    return before, after


def per_device(
    displacement,
    cell_scale,
    material_id,
    stiff_table,
    mass_table,
    pile_block,
    pile_owner,
    node_index,
):
    planes, ny, nz = cell_scale.shape
    rows = planes * ny
    tiles = lax.axis_size("tile")
    _, block_count, width = node_index.shape
    order = pile_block.shape[-1]
    blocks = tiles * block_count
    vmem = pl.BlockSpec(memory_space=pltpu.VMEM)
    smem = pl.BlockSpec(memory_space=pltpu.SMEM)
    big = pltpu.CompilerParams(vmem_limit_bytes=32 * 1024 * 1024)
    field = displacement.reshape(6, planes, ny, nz)
    nodes = node_index.transpose(1, 0, 2).reshape(blocks, width)
    owner = pile_owner.reshape(1, tiles)
    payload, slot_row, slot_column, info = pl.pallas_call(
        functools.partial(gather_kernel, tiles),
        out_shape=(
            jax.ShapeDtypeStruct((tiles, 2 * order), BF16),
            jax.ShapeDtypeStruct((MOST, width), I32),
            jax.ShapeDtypeStruct((MOST, width), I32),
            jax.ShapeDtypeStruct((2 * MOST, width), I32),
        ),
        in_specs=[vmem] * 3,
        out_specs=(vmem,) * 4,
        scratch_shapes=[pltpu.VMEM((MOST, 6 * width), F32)],
        compiler_params=big,
        cost_estimate=pl.CostEstimate(flops=10**9, bytes_accessed=10**6, transcendentals=0),
        name="gather",
    )(displacement.reshape(6, rows, nz), nodes, owner)
    arrived = lax.all_to_all(payload.reshape(tiles, 2, order), "tile", 0, 0, tiled=True)
    before, after = halos(field, cell_scale, material_id)
    soil = pl.pallas_call(
        soil_kernel,
        out_shape=jax.ShapeDtypeStruct(field.shape, F32),
        in_specs=[vmem] * 5 + [smem] * 2,
        out_specs=vmem,
        compiler_params=big,
        cost_estimate=pl.CostEstimate(flops=10**7, bytes_accessed=10**7, transcendentals=0),
        name="soil",
    )(field, cell_scale, material_id, before, after, stiff_table, mass_table)
    returning = pl.pallas_call(
        pile_kernel,
        out_shape=jax.ShapeDtypeStruct((tiles, 2 * order), BF16),
        in_specs=[vmem] * 3,
        out_specs=vmem,
        compiler_params=big,
        cost_estimate=pl.CostEstimate(flops=10**8, bytes_accessed=6 * 10**6, transcendentals=0),
        name="pile",
    )(arrived, pile_block[0], info)
    landed = lax.all_to_all(returning.reshape(tiles, 2, order), "tile", 0, 0, tiled=True)
    result = pl.pallas_call(
        functools.partial(scatter_kernel, tiles),
        out_shape=jax.ShapeDtypeStruct((6, rows, nz), F32),
        in_specs=[vmem] * 4 + [smem],
        out_specs=vmem,
        scratch_shapes=[pltpu.VMEM((6 * rows, MOST * width), BF16)],
        compiler_params=big,
        cost_estimate=pl.CostEstimate(flops=10**9, bytes_accessed=2 * 10**6, transcendentals=0),
        name="scatter",
    )(soil.reshape(6, rows, nz), landed, slot_row, slot_column, info)
    return result.reshape(displacement.shape)


def solution(mesh):
    placed = (
        P(None, None, ("freq", "tile"), None, None),
        P("tile", None, None),
        P("tile", None, None),
        P(None, "freq"),
        P(None, "freq"),
        P(("freq", "tile"), None, None, None),
        P("freq"),
        P(),
    )
    return jax.shard_map(
        per_device,
        mesh=mesh,
        in_specs=placed,
        out_specs=P(None, None, ("freq", "tile"), None, None),
        check_vma=False,
    )
```

```python
import functools

import jax
import jax.numpy as jnp
from jax import lax
from jax.experimental import pallas as pl
from jax.experimental.pallas import tpu as pltpu
from jax.sharding import PartitionSpec as P

MOST = 8
F32 = jnp.float32
BF16 = jnp.bfloat16
I32 = jnp.int32
NT = (((1,), (1,)), ((), ()))


def iota(shape, axis):
    return lax.broadcasted_iota(I32, shape, axis)


def onehot(mask):
    return jnp.where(mask, 1.0, 0.0).astype(BF16)


def dot(left, right):
    return jnp.dot(left, right, preferred_element_type=F32)


def dot_nt(left, right):
    return lax.dot_general(left, right, NT, preferred_element_type=F32)


def slots_of(nodes, me, cells, columns):
    blocks, width = nodes.shape
    local = nodes - me * cells
    inside = (local >= 0) & (local < cells)
    shift = columns.bit_length() - 1
    row1 = jnp.where(inside, (local >> shift) + 1, 0).astype(F32).astype(BF16)
    column = jnp.where(inside, local & (columns - 1), 0).astype(F32).astype(BF16)
    first = onehot(iota((MOST, width), 1) == 0)
    onto = dot_nt(first, onehot(inside))
    upper = onehot(iota((blocks, blocks), 0) < iota((blocks, blocks), 1))
    rank = dot(onto.astype(BF16), upper)
    slot = (onto > 0.5) & (rank == iota((MOST, blocks), 0).astype(F32))
    chosen = onehot(slot)
    return slot, dot(chosen, row1).astype(I32) - 1, dot(chosen, column).astype(I32)


def gather_kernel(
    tiles,
    displacement_hbm,
    nodes_hbm,
    owner_hbm,
    picked_ref,
    info_ref,
    displacement,
    node_buffer,
    owner_buffer,
    semaphores,
):
    me = lax.axis_index("tile")
    copies = [
        pltpu.make_async_copy(source, target, semaphores.at[i])
        for i, (source, target) in enumerate(
            ((nodes_hbm, node_buffer), (owner_hbm, owner_buffer), (displacement_hbm, displacement))
        )
    ]
    for copy in copies:
        copy.start()
    copies[0].wait()
    copies[1].wait()
    components, rows, columns = displacement.shape
    blocks, width = node_buffer.shape
    block_count = blocks // tiles
    nodes = node_buffer[...]
    owner = owner_buffer[...]
    cells = rows * columns
    slot, slot_row, slot_column = slots_of(nodes, me, cells, columns)
    twin_slot, _, _ = slots_of(nodes, me ^ 1, cells, columns)
    target = jnp.concatenate([owner + (b * tiles + 1) for b in range(block_count)], axis=1)
    for i, chosen in enumerate((slot, twin_slot)):
        one = jnp.sum(jnp.where(chosen, target.astype(F32), 0.0), axis=1, keepdims=True).astype(I32) - 1
        info_ref[i * MOST : (i + 1) * MOST, :] = jnp.broadcast_to(one, (MOST, width))
    info_ref[2 * MOST :, :] = jnp.zeros((MOST, width), I32)
    first = onehot(iota((MOST, width), 1) == 0)
    tile_of = jnp.floor(((nodes >> 13).astype(F32) + 0.5) * (1.0 / (cells >> 13)))
    tile_row = dot_nt(first, tile_of.astype(BF16))[0:1, :]
    for b in range(block_count):
        own = jnp.where(owner == me, tile_row[:, b * tiles : (b + 1) * tiles], 0.0)
        info_ref[2 * MOST + b : 2 * MOST + b + 1, :] = jnp.broadcast_to(
            jnp.sum(own, axis=1, keepdims=True).astype(I32), (1, width)
        )
    copies[2].wait()
    field = displacement[...].reshape(components * rows, columns).astype(BF16)
    empty = jnp.zeros((8 - components, width), F32)
    for pair in range(MOST // 2):
        at_column = jnp.concatenate(
            [
                onehot(iota((columns, width), 0) == slot_column[s : s + 1, :])
                for s in (2 * pair, 2 * pair + 1)
            ],
            axis=1,
        )
        taken = dot(field, at_column)
        for i in range(2):
            s = 2 * pair + i
            at_row = iota((rows, width), 0) == slot_row[s : s + 1, :]
            found = []
            for c in range(components):
                one = taken[c * rows : (c + 1) * rows, i * width : (i + 1) * width]
                found.append(jnp.sum(jnp.where(at_row, one, 0.0), axis=0, keepdims=True))
            picked_ref[s] = jnp.concatenate(found + [empty], axis=0).astype(BF16)


def codes_in_lanes(targets, tiles, core, block_count, width):
    owner = targets & (tiles - 1)
    code = ((owner >> 1) * block_count + (targets >> (tiles.bit_length() - 1))) * 8
    code = jnp.where((targets >= 0) & ((owner & 1) == core), code, -width)
    count = targets.shape[0]
    lane = iota((count, width), 1)
    code = jnp.where((lane >> 3) == iota((count, width), 0), code + (lane & 7), 0)
    return jnp.sum(code, axis=0, keepdims=True)


def place_kernel(tiles, picked_ref, twin_ref, info_ref, payload_ref):
    core = lax.axis_index("tile") & 1
    chips, block_count, padded, width = payload_ref.shape
    code = codes_in_lanes(info_ref[0 : 2 * MOST, :], tiles, core, block_count, width)
    place = onehot(iota((chips * block_count * padded, width), 0) == code)
    picked = jnp.concatenate([picked_ref[...].reshape(MOST * 8, width), twin_ref[...].reshape(MOST * 8, width)], axis=0)
    payload_ref[...] = dot(place, picked).astype(BF16).reshape(payload_ref.shape)


def pile_kernel(arrived_ref, imag_ref, block_hbm, info_ref, order_ref, payload_ref, real_ref, semaphores):
    chips, block_count, padded, width = arrived_ref.shape
    components = 6
    half = components // 2
    part = real_ref.shape[0] // half
    copies = []
    for c in range(half):
        rows = slice(c * part, (c + 1) * part)
        copies.append(pltpu.make_async_copy(block_hbm.at[0, rows], real_ref.at[rows], semaphores.at[c]))
        copies[c].start()
    vector = jnp.sum(arrived_ref[...].astype(F32), axis=0)
    vector = jnp.concatenate(
        [
            jnp.concatenate(
                [vector[b, i * half + c : i * half + c + 1, :] for c in range(half) for b in range(block_count)], axis=1
            )
            for i in range(2)
        ],
        axis=0,
    ).astype(BF16)
    by_imag = dot_nt(vector, imag_ref[...])
    real, imag = [], []
    for c in range(half):
        rows = slice(c * part, (c + 1) * part)
        copies[c].wait()
        by_real = dot_nt(vector, real_ref[rows, :])
        real.append(by_real[0:1] - by_imag[1:2, rows])
        imag.append(by_real[1:2] + by_imag[0:1, rows])
    empty = jnp.zeros((padded - components, width), F32)
    for b in range(block_count):
        piece = [one[:, b * width : (b + 1) * width] for one in real + imag]
        piece = jnp.concatenate(piece + [empty], axis=0)
        chip = info_ref[2 * MOST + b : 2 * MOST + b + 1, :] >> 1
        for k in range(chips):
            payload_ref[k, b] = jnp.where(chip == k, piece, 0.0).astype(BF16)


def choose_kernel(tiles, landed_ref, info_ref, order_ref, own_ref, twin_ref):
    core = lax.axis_index("tile") & 1
    chips, block_count, padded, width = landed_ref.shape
    slab = chips * block_count * padded
    targets = info_ref[0 : 2 * MOST, :]
    owner = targets & (tiles - 1)
    code = ((owner >> 1) * block_count + (targets >> (tiles.bit_length() - 1))) * padded
    code = jnp.where((targets >= 0) & ((owner & 1) == core), code, -padded)
    shape = (2 * MOST, padded, slab)
    take = onehot(iota(shape, 2) == code[:, 0:1].reshape(2 * MOST, 1, 1) + iota(shape, 1))
    chosen = dot(take.reshape(2 * MOST * padded, slab), landed_ref[...].reshape(slab, width)).astype(BF16)
    chosen = chosen.reshape(2, MOST, padded, width)
    own_ref[...] = chosen[0]
    twin_ref[...] = chosen[1]


def scatter_kernel(soil_ref, own_ref, twin_ref, row_ref, at_column_ref, result_ref, spread):
    components, rows, columns = soil_ref.shape
    width = row_ref.shape[1]
    for s in range(MOST):
        piece = own_ref[s].astype(F32) + twin_ref[s].astype(F32)
        at_row = iota((rows, width), 0) == row_ref[s : s + 1, :]
        for k in range(components):
            spread[k * rows : (k + 1) * rows, s * width : (s + 1) * width] = jnp.where(
                at_row, piece[k : k + 1, :], 0.0
            ).astype(BF16)
    added = dot_nt(spread[...], at_column_ref[...])
    result_ref[...] = soil_ref[...] + added.reshape(components, rows, columns)


def fetch_kernel(after_ref, block_hbm, imag_ref, semaphore):
    copy = pltpu.make_async_copy(block_hbm.at[1], imag_ref, semaphore)
    copy.start()
    copy.wait()


def plane_kernel(last, order_ref, displacement_hbm, scale_hbm, kind_hbm, plane_ref, kind, semaphores):
    planes = scale_hbm.shape[0]
    x = jnp.where((lax.axis_index("tile") & 1) == last, planes - 1, 0)
    sources = (kind_hbm.at[x], scale_hbm.at[x], displacement_hbm.at[:, x])
    targets = (kind, plane_ref.at[6], plane_ref.at[0:6])
    copies = [pltpu.make_async_copy(*two, semaphores.at[i]) for i, two in enumerate(zip(sources, targets))]
    for copy in copies:
        copy.start()
    copies[0].wait()
    plane_ref[7] = kind[...].astype(F32)
    for copy in copies[1:]:
        copy.wait()


def lookup(table_ref, row, kind):
    bits = [(kind & (1 << k)) != 0 for k in range(4)]
    level = [table_ref[row, k] for k in range(16)]
    for bit in bits:
        level = [jnp.where(bit, level[2 * k + 1], level[2 * k]) for k in range(len(level) // 2)]
    return level[0]


def half_stiffness(table_ref, kind, scale):
    return [0.5 * (lookup(table_ref, i, kind) * scale) for i in range(2)]


def flux(face, near, far):
    strain = [near[k] - far[k] for k in range(6)]
    real = [face[0] * strain[c] - face[1] * strain[3 + c] for c in range(3)]
    imag = [face[0] * strain[3 + c] + face[1] * strain[c] for c in range(3)]
    return real + imag


def soil_kernel(
    order_ref,
    displacement_hbm,
    scale_hbm,
    kind_hbm,
    near_hbm,
    nodes_hbm,
    stiff_ref,
    mass_ref,
    soil_ref,
    edge_ref,
    row_ref,
    at_column_ref,
    displacement_ref,
    scale_ref,
    kind_ref,
    near_ref,
    node_buffer,
    semaphores,
):
    sources = (nodes_hbm, kind_hbm, scale_hbm, displacement_hbm, near_hbm)
    targets = (node_buffer, kind_ref, scale_ref, displacement_ref, near_ref)
    copies = [pltpu.make_async_copy(*two, semaphores.at[i]) for i, two in enumerate(zip(sources, targets))]
    for copy in copies:
        copy.start()
    _, planes, ny, nz = displacement_ref.shape
    shape = (ny, nz)
    tile = lax.axis_index("tile")
    odd = tile & 1
    even = odd == 0
    copies[0].wait()
    width = node_buffer.shape[1]
    _, row_ref[...], slot_column = slots_of(node_buffer[...], tile, planes * ny * nz, nz)
    for s in range(MOST):
        at_column = onehot(iota((nz, width), 0) == slot_column[s : s + 1, :])
        at_column_ref[:, s * width : (s + 1) * width] = at_column
    for copy in copies[1:]:
        copy.wait()
    at_y, at_z = iota(shape, 0), iota(shape, 1)
    y_last, z_last = at_y == ny - 1, at_z == nz - 1
    edges = (
        jnp.where(at_y == 0, 0.5, 0.0)
        + jnp.where(y_last, 0.5, 0.0)
        + jnp.where(at_z == 0, 0.5, 0.0)
        + jnp.where(z_last, 0.5, 0.0)
    )
    half = [half_stiffness(stiff_ref, kind_ref[x], scale_ref[x]) for x in range(planes)]
    near_half = half_stiffness(stiff_ref, near_ref[7].astype(I32), near_ref[6])
    near = [near_ref[k] for k in range(6)]
    fields = [[displacement_ref[k, x] for k in range(6)] for x in range(planes)]

    def chosen(first, last, flag):
        return [jnp.where(flag, b, a) for a, b in zip(first, last)]

    beside = chosen(fields[0], fields[-1], even)
    beside_half = chosen(half[0], half[-1], even)
    near_flux = flux([beside_half[i] + near_half[i] for i in range(2)], beside, near)
    outer = chosen(fields[0] + half[0], fields[-1] + half[-1], jnp.logical_not(even))
    for k in range(8):
        edge_ref[k] = outer[k]
    before = [0.0] * 6
    for x in range(planes):
        u, own = fields[x], half[x]
        diagonal = [lookup(mass_ref, i, kind_ref[x]) + 2.0 * edges * own[i] for i in range(2)]
        total = [diagonal[0] * u[c] - diagonal[1] * u[3 + c] for c in range(3)]
        total += [diagonal[0] * u[3 + c] + diagonal[1] * u[c] for c in range(3)]
        total = [total[k] - before[k] for k in range(6)]
        if x < planes - 1:
            before = flux([own[i] + half[x + 1][i] for i in range(2)], u, fields[x + 1])
            total = [total[k] + before[k] for k in range(6)]
        for axis, last in ((0, y_last), (1, z_last)):
            size = shape[axis]
            face = [jnp.where(last, 0.0, own[i] + pltpu.roll(own[i], size - 1, axis)) for i in range(2)]
            next_to = [pltpu.roll(u[k], size - 1, axis) for k in range(6)]
            along = flux(face, u, next_to)
            total = [total[k] + along[k] - pltpu.roll(along[k], 1, axis) for k in range(6)]
        if x in (0, planes - 1):
            total = [jnp.where(even == (x == planes - 1), total[k] + near_flux[k], total[k]) for k in range(6)]
        for k in range(6):
            soil_ref[k, x] = total[k]


def outer_kernel(soil_ref, edge_ref, far_ref, stiff_ref, result_ref):
    planes = result_ref.shape[1]
    far_half = half_stiffness(stiff_ref, far_ref[7].astype(I32), far_ref[6])
    face = [edge_ref[6 + i] + far_half[i] for i in range(2)]
    along = flux(face, [edge_ref[k] for k in range(6)], [far_ref[k] for k in range(6)])
    x = (lax.axis_index("tile") & 1) * (planes - 1)
    for k in range(6):
        result_ref[k, x] = soil_ref[k, x] + along[k]


def per_device(
    displacement,
    cell_scale,
    material_id,
    stiff_table,
    mass_table,
    pile_block,
    pile_owner,
    node_index,
):
    planes, ny, nz = cell_scale.shape
    rows = planes * ny
    tiles = lax.axis_size("tile")
    chips = tiles // 2
    _, block_count, width = node_index.shape
    blocks = tiles * block_count
    vmem = pl.BlockSpec(memory_space=pltpu.VMEM)
    smem = pl.BlockSpec(memory_space=pltpu.SMEM)
    hbm = pl.BlockSpec(memory_space=pltpu.HBM)
    anywhere = pl.BlockSpec(memory_space=pl.ANY)
    dma = pltpu.SemaphoreType.DMA

    def call(kernel, name, out_shape, in_specs, scratch=(), flops=10**8, moved=10**6):
        return pl.pallas_call(
            kernel,
            out_shape=out_shape,
            in_specs=in_specs,
            out_specs=jax.tree.map(lambda _: vmem, out_shape),
            scratch_shapes=list(scratch),
            compiler_params=pltpu.CompilerParams(vmem_limit_bytes=16 * 1024 * 1024),
            cost_estimate=pl.CostEstimate(flops=flops, bytes_accessed=moved, transcendentals=0),
            name=name,
        )

    def in_hbm(array):
        return pltpu.with_memory_space_constraint(array, pltpu.HBM)

    def shape(dims, kind):
        return jax.ShapeDtypeStruct(dims, kind)

    field = displacement.reshape(6, planes, ny, nz)
    nodes = node_index.transpose(1, 0, 2).reshape(blocks, width)
    owner = pile_owner.reshape(1, tiles)
    slab = (chips, block_count, 8, width)
    pair = [(i, i ^ 1) for i in range(tiles)]
    groups = [[2 * chip + core for chip in range(chips)] for core in range(2)]

    def exchange(payload):
        return lax.all_to_all(payload, "tile", 0, 0, axis_index_groups=groups, tiled=True)

    picked, info = call(
        functools.partial(gather_kernel, tiles),
        "gather",
        (
            shape((MOST, 8, width), BF16),
            shape((3 * MOST, width), I32),
        ),
        [hbm] * 3,
        [
            pltpu.VMEM((6, rows, nz), F32),
            pltpu.VMEM((blocks, width), I32),
            pltpu.VMEM((1, tiles), I32),
            dma((3,)),
        ],
    )(in_hbm(displacement.reshape(6, rows, nz)), in_hbm(nodes), in_hbm(owner))
    payload = call(functools.partial(place_kernel, tiles), "place", shape(slab, BF16), [vmem] * 3)(
        picked, lax.ppermute(picked, "tile", pair), info
    )
    arrived = exchange(payload)

    size = (8, ny, nz)

    def plane(last, order):
        return call(
            functools.partial(plane_kernel, last),
            "plane",
            shape(size, F32),
            [anywhere] + [hbm] * 3,
            [pltpu.VMEM((ny, nz), I32), dma((3,))],
        )(order, in_hbm(field), in_hbm(cell_scale), in_hbm(material_id))

    to_near = plane(0, payload)
    near = lax.ppermute(to_near, "tile", pair)
    order = pile_block.shape[-1]
    block = in_hbm(pile_block.reshape(2, order, order))
    square = (order, order)
    imag = call(fetch_kernel, "fetch", shape(square, BF16), [anywhere, hbm], [dma], flops=10**11, moved=10**8)(to_near, block)
    returning = call(
        pile_kernel,
        "pile",
        shape(slab, BF16),
        [vmem, vmem, hbm, vmem, anywhere],
        [pltpu.VMEM(square, BF16), dma((3,))],
    )(arrived, imag, block, info, near)
    landed = exchange(returning)
    next_chip = [(i, i + 1) for i in range(1, tiles - 1, 2)]
    far = lax.ppermute(plane(1, returning), "tile", next_chip + [(j, i) for i, j in next_chip])

    soil, edge, slot_row, at_column = call(
        soil_kernel,
        "soil",
        (shape(field.shape, F32), shape(size, F32), shape((MOST, width), I32), shape((nz, MOST * width), BF16)),
        [anywhere] + [hbm] * 5 + [smem] * 2,
        [
            pltpu.VMEM(field.shape, F32),
            pltpu.VMEM(cell_scale.shape, F32),
            pltpu.VMEM(cell_scale.shape, I32),
            pltpu.VMEM(size, F32),
            pltpu.VMEM((blocks, width), I32),
            dma((5,)),
        ],
        flops=10**11,
        moved=10**7,
    )(returning, *map(in_hbm, (field, cell_scale, material_id, near, nodes)), stiff_table, mass_table)
    slots = shape((MOST, 8, width), BF16)
    own, twin = call(functools.partial(choose_kernel, tiles), "choose", (slots, slots), [vmem] * 2 + [anywhere])(
        landed, info, soil
    )
    twin = lax.ppermute(twin, "tile", pair)
    soil = pl.pallas_call(
        outer_kernel,
        out_shape=shape(field.shape, F32),
        in_specs=[vmem] * 3 + [smem],
        out_specs=vmem,
        input_output_aliases={0: 0},
        compiler_params=pltpu.CompilerParams(vmem_limit_bytes=16 * 1024 * 1024),
        cost_estimate=pl.CostEstimate(flops=10**10, bytes_accessed=10**6, transcendentals=0),
        name="outer",
    )(soil, edge, far, stiff_table)
    result = call(
        scatter_kernel,
        "scatter",
        shape((6, rows, nz), F32),
        [vmem] * 5,
        [pltpu.VMEM((6 * rows, MOST * width), BF16)],
    )(soil.reshape(6, rows, nz), own, twin, slot_row, at_column)
    return result.reshape(displacement.shape)


def solution(mesh):
    placed = (
        P(None, None, ("freq", "tile"), None, None),
        P("tile", None, None),
        P("tile", None, None),
        P(None, "freq"),
        P(None, "freq"),
        P(("freq", "tile"), None, None, None),
        P("freq"),
        P(),
    )
    return jax.shard_map(
        per_device,
        mesh=mesh,
        in_specs=placed,
        out_specs=P(None, None, ("freq", "tile"), None, None),
        check_vma=False,
    )
```

```python
import functools

import jax
import jax.numpy as jnp
from jax import lax
from jax.experimental import pallas as pl
from jax.experimental.pallas import tpu as pltpu
from jax.sharding import PartitionSpec as P

MOST = 8
F32 = jnp.float32
BF16 = jnp.bfloat16
I32 = jnp.int32
NT = (((1,), (1,)), ((), ()))


def iota(shape, axis):
    return lax.broadcasted_iota(I32, shape, axis)


def onehot(mask):
    return jnp.where(mask, 1.0, 0.0).astype(BF16)


def dot(left, right):
    return jnp.dot(left, right, preferred_element_type=F32)


def dot_nt(left, right):
    return lax.dot_general(left, right, NT, preferred_element_type=F32)


def slots_of(nodes, me, cells, columns):
    blocks, width = nodes.shape
    local = nodes - me * cells
    inside = (local >= 0) & (local < cells)
    shift = columns.bit_length() - 1
    row1 = jnp.where(inside, (local >> shift) + 1, 0).astype(F32).astype(BF16)
    column = jnp.where(inside, local & (columns - 1), 0).astype(F32).astype(BF16)
    first = onehot(iota((MOST, width), 1) == 0)
    onto = dot_nt(first, onehot(inside))
    upper = onehot(iota((blocks, blocks), 0) < iota((blocks, blocks), 1))
    rank = dot(onto.astype(BF16), upper)
    slot = (onto > 0.5) & (rank == iota((MOST, blocks), 0).astype(F32))
    chosen = onehot(slot)
    return slot, dot(chosen, row1).astype(I32) - 1, dot(chosen, column).astype(I32)


def gather_kernel(
    tiles,
    displacement_hbm,
    nodes_hbm,
    owner_hbm,
    picked_ref,
    info_ref,
    displacement,
    node_buffer,
    owner_buffer,
    semaphores,
):
    me = lax.axis_index("tile")
    copies = [
        pltpu.make_async_copy(source, target, semaphores.at[i])
        for i, (source, target) in enumerate(
            ((nodes_hbm, node_buffer), (owner_hbm, owner_buffer), (displacement_hbm, displacement))
        )
    ]
    for copy in copies:
        copy.start()
    copies[0].wait()
    copies[1].wait()
    components, rows, columns = displacement.shape
    blocks, width = node_buffer.shape
    block_count = blocks // tiles
    nodes = node_buffer[...]
    owner = owner_buffer[...]
    cells = rows * columns
    slot, slot_row, slot_column = slots_of(nodes, me, cells, columns)
    twin_slot, _, _ = slots_of(nodes, me ^ 1, cells, columns)
    target = jnp.concatenate([owner + (b * tiles + 1) for b in range(block_count)], axis=1)
    for i, chosen in enumerate((slot, twin_slot)):
        one = jnp.sum(jnp.where(chosen, target.astype(F32), 0.0), axis=1, keepdims=True).astype(I32) - 1
        info_ref[i * MOST : (i + 1) * MOST, :] = jnp.broadcast_to(one, (MOST, width))
    info_ref[2 * MOST :, :] = jnp.zeros((MOST, width), I32)
    first = onehot(iota((MOST, width), 1) == 0)
    tile_of = jnp.floor(((nodes >> 13).astype(F32) + 0.5) * (1.0 / (cells >> 13)))
    tile_row = dot_nt(first, tile_of.astype(BF16))[0:1, :]
    for b in range(block_count):
        own = jnp.where(owner == me, tile_row[:, b * tiles : (b + 1) * tiles], 0.0)
        info_ref[2 * MOST + b : 2 * MOST + b + 1, :] = jnp.broadcast_to(
            jnp.sum(own, axis=1, keepdims=True).astype(I32), (1, width)
        )
    copies[2].wait()
    field = displacement[...].reshape(components * rows, columns).astype(BF16)
    empty = jnp.zeros((8 - components, width), F32)
    for pair in range(MOST // 2):
        at_column = jnp.concatenate(
            [
                onehot(iota((columns, width), 0) == slot_column[s : s + 1, :])
                for s in (2 * pair, 2 * pair + 1)
            ],
            axis=1,
        )
        taken = dot(field, at_column)
        for i in range(2):
            s = 2 * pair + i
            at_row = iota((rows, width), 0) == slot_row[s : s + 1, :]
            found = []
            for r in range(components):
                k = component(r)
                one = taken[k * rows : (k + 1) * rows, i * width : (i + 1) * width]
                found.append(jnp.sum(jnp.where(at_row, one, 0.0), axis=0, keepdims=True))
            picked_ref[s] = jnp.concatenate(found + [empty], axis=0).astype(BF16)


def component(row):
    return (row & 1) * 3 + (row >> 1)


def payload_rows(targets, row, tiles, core):
    owner = targets & (tiles - 1)
    block = targets >> (tiles.bit_length() - 1)
    code = (owner >> 1) * 18 + block * 2 + (row >> 1) * 6 + (row & 1)
    return jnp.where((targets >= 0) & ((owner & 1) == core) & (row < 6), code, -1)


def place_kernel(tiles, picked_ref, twin_ref, info_ref, payload_ref):
    core = lax.axis_index("tile") & 1
    rows, width = payload_ref.shape
    lane = iota((2 * MOST, width), 1)
    code = payload_rows(info_ref[0 : 2 * MOST, :], lane & 7, tiles, core)
    code = jnp.sum(jnp.where((lane >> 3) == iota((2 * MOST, width), 0), code, 0), axis=0, keepdims=True)
    place = onehot(iota((rows, width), 0) == code)
    picked = jnp.concatenate([picked_ref[...].reshape(MOST * 8, width), twin_ref[...].reshape(MOST * 8, width)], axis=0)
    payload_ref[...] = dot(place, picked).astype(BF16)


def pile_kernel(arrived_ref, imag_ref, more_ref, block_hbm, info_ref, order_ref, payload_ref, real_ref, semaphores):
    rows, width = payload_ref.shape
    _, pieces, _, _ = arrived_ref.shape
    order = imag_ref.shape[0]
    ahead = more_ref.shape[0]
    ends = (ahead, 640, order)
    copies = []
    for i, (start, stop) in enumerate(zip(ends, ends[1:])):
        copies.append(pltpu.make_async_copy(block_hbm.at[0, start:stop], real_ref.at[start:stop], semaphores.at[i]))
        copies[i].start()
    vector = jnp.sum(arrived_ref[...].astype(F32), axis=0)
    vector = jnp.concatenate([vector[k] for k in range(pieces)], axis=1).astype(BF16)
    by_imag = dot_nt(vector, imag_ref[...])
    by_real = [dot_nt(vector, more_ref[...])]
    for i, (start, stop) in enumerate(zip(ends, ends[1:])):
        copies[i].wait()
        by_real.append(dot_nt(vector, real_ref[start:stop, :]))
    by_real = jnp.concatenate(by_real, axis=1)
    real = by_real[0:1] - by_imag[1:2]
    imag = by_real[1:2] + by_imag[0:1]
    traction = [part[:, k * width : (k + 1) * width] for k in range(pieces) for part in (real, imag)]
    traction = jnp.concatenate(traction + [jnp.zeros((width - 2 * pieces, width), F32)], axis=0).astype(BF16)
    lane = iota((1, width), 1)
    block = (lane >> 1) % 3
    chip = info_ref[2 * MOST : 2 * MOST + 1, :] >> 1
    for b in (1, 2):
        chip = jnp.where(block == b, info_ref[2 * MOST + b : 2 * MOST + b + 1, :] >> 1, chip)
    code = jnp.where(lane < 2 * pieces, chip * (2 * pieces) + lane, -1)
    place = onehot(iota((rows, width), 0) == code)
    payload_ref[...] = dot(place, traction).astype(BF16)


def choose_kernel(tiles, landed_ref, info_ref, order_ref, own_ref, twin_ref):
    core = lax.axis_index("tile") & 1
    slab, width = landed_ref.shape
    count = 2 * MOST
    shape = (count, 8, slab)
    targets = info_ref[0:count, 0:1].reshape(count, 1, 1)
    code = payload_rows(targets, iota((count, 8, 1), 1), tiles, core)
    take = onehot(iota(shape, 2) == code).reshape(count * 8, slab)
    chosen = dot(take, landed_ref[...]).astype(BF16).reshape(2, MOST, 8, width)
    own_ref[...] = chosen[0]
    twin_ref[...] = chosen[1]


def scatter_kernel(soil_ref, own_ref, twin_ref, row_ref, at_column_ref, result_ref, spread):
    components, rows, columns = soil_ref.shape
    width = row_ref.shape[1]
    for s in range(MOST):
        piece = own_ref[s].astype(F32) + twin_ref[s].astype(F32)
        at_row = iota((rows, width), 0) == row_ref[s : s + 1, :]
        for r in range(components):
            k = component(r)
            spread[k * rows : (k + 1) * rows, s * width : (s + 1) * width] = jnp.where(
                at_row, piece[r : r + 1, :], 0.0
            ).astype(BF16)
    added = dot_nt(spread[...], at_column_ref[...])
    result_ref[...] = soil_ref[...] + added.reshape(components, rows, columns)


def ahead_kernel(
    order_ref,
    displacement_hbm,
    scale_hbm,
    kind_hbm,
    block_hbm,
    near_hbm,
    far_hbm,
    imag_ref,
    more_ref,
    near,
    far,
    kind,
    semaphores,
):
    planes = scale_hbm.shape[0]
    odd = lax.axis_index("tile") & 1
    sides = ((near, near_hbm, (1 - odd) * (planes - 1)), (far, far_hbm, odd * (planes - 1)))
    pairs = [(kind_hbm, kind)]
    for plane, _, x in sides:
        pairs += [(displacement_hbm.at[:, x], plane.at[0:6]), (scale_hbm.at[x], plane.at[6])]
    pairs += [(block_hbm.at[1], imag_ref), (block_hbm.at[0, 0 : more_ref.shape[0]], more_ref)]
    copies = [pltpu.make_async_copy(*pair, semaphores.at[i]) for i, pair in enumerate(pairs)]
    for copy in copies:
        copy.start()
    copies[0].wait()
    for plane, _, x in sides:
        plane[7] = kind[x].astype(F32)
    for i, (plane, target, _) in enumerate(sides):
        copies[2 * i + 1].wait()
        copies[2 * i + 2].wait()
        copies.append(pltpu.make_async_copy(plane, target, semaphores.at[7 + i]))
        copies[-1].start()
    for copy in copies[5:]:
        copy.wait()


def token_kernel(order_ref, token_ref):
    token_ref[...] = jnp.zeros(token_ref.shape, F32)


def lookup(table_ref, row, kind):
    bits = [(kind & (1 << k)) != 0 for k in range(4)]
    level = [table_ref[row, k] for k in range(16)]
    for bit in bits:
        level = [jnp.where(bit, level[2 * k + 1], level[2 * k]) for k in range(len(level) // 2)]
    return level[0]


def half_stiffness(table_ref, kind, scale):
    return [0.5 * (lookup(table_ref, i, kind) * scale) for i in range(2)]


def flux(face, near, far):
    strain = [near[k] - far[k] for k in range(6)]
    real = [face[0] * strain[c] - face[1] * strain[3 + c] for c in range(3)]
    imag = [face[0] * strain[3 + c] + face[1] * strain[c] for c in range(3)]
    return real + imag


def soil_kernel(
    tiles,
    order_ref,
    displacement_hbm,
    scale_hbm,
    kind_hbm,
    near_hbm,
    far_hbm,
    nodes_hbm,
    stiff_ref,
    mass_ref,
    soil_ref,
    row_ref,
    at_column_ref,
    displacement_ref,
    scale_ref,
    kind_ref,
    near_ref,
    far_ref,
    node_buffer,
    semaphores,
):
    sources = (nodes_hbm, kind_hbm, scale_hbm, displacement_hbm, near_hbm, far_hbm)
    targets = (node_buffer, kind_ref, scale_ref, displacement_ref, near_ref, far_ref)
    copies = [pltpu.make_async_copy(*two, semaphores.at[i]) for i, two in enumerate(zip(sources, targets))]
    for copy in copies:
        copy.start()
    _, planes, ny, nz = displacement_ref.shape
    shape = (ny, nz)
    tile = lax.axis_index("tile")
    odd = tile & 1
    even = odd == 0
    copies[0].wait()
    width = node_buffer.shape[1]
    _, row_ref[...], slot_column = slots_of(node_buffer[...], tile, planes * ny * nz, nz)
    for s in range(MOST):
        at_column = onehot(iota((nz, width), 0) == slot_column[s : s + 1, :])
        at_column_ref[:, s * width : (s + 1) * width] = at_column
    for copy in copies[1:]:
        copy.wait()

    @pl.when((tile == 0) | (tile == tiles - 1))
    def _():
        far_ref[...] = jnp.zeros(far_ref.shape, F32)

    at_y, at_z = iota(shape, 0), iota(shape, 1)
    y_last, z_last = at_y == ny - 1, at_z == nz - 1
    edges = (
        jnp.where(at_y == 0, 0.5, 0.0)
        + jnp.where(y_last, 0.5, 0.0)
        + jnp.where(at_z == 0, 0.5, 0.0)
        + jnp.where(z_last, 0.5, 0.0)
    )
    half = [half_stiffness(stiff_ref, kind_ref[x], scale_ref[x]) for x in range(planes)]
    fields = [[displacement_ref[k, x] for k in range(6)] for x in range(planes)]

    def outside(first, second, flag):
        return [jnp.where(flag, first[k], second[k]) for k in range(6)], [
            jnp.where(flag, a, b)
            for a, b in zip(*(half_stiffness(stiff_ref, ref[7].astype(I32), ref[6]) for ref in (first, second)))
        ]

    before, before_half = outside(far_ref, near_ref, even)
    after, after_half = outside(near_ref, far_ref, even)
    fields = [before] + fields + [after]
    half = [before_half] + half + [after_half]

    def x_flux(x):
        return flux([half[x][i] + half[x + 1][i] for i in range(2)], fields[x], fields[x + 1])

    before = x_flux(0)
    for x in range(planes):
        u, own = fields[x + 1], half[x + 1]
        diagonal = [lookup(mass_ref, i, kind_ref[x]) + 2.0 * edges * own[i] for i in range(2)]
        total = [diagonal[0] * u[c] - diagonal[1] * u[3 + c] for c in range(3)]
        total += [diagonal[0] * u[3 + c] + diagonal[1] * u[c] for c in range(3)]
        beyond = x_flux(x + 1)
        total = [total[k] + beyond[k] - before[k] for k in range(6)]
        before = beyond
        for axis, last in ((0, y_last), (1, z_last)):
            size = shape[axis]
            face = [jnp.where(last, 0.0, own[i] + pltpu.roll(own[i], size - 1, axis)) for i in range(2)]
            next_to = [pltpu.roll(u[k], size - 1, axis) for k in range(6)]
            along = flux(face, u, next_to)
            total = [total[k] + along[k] - pltpu.roll(along[k], 1, axis) for k in range(6)]
        for k in range(6):
            soil_ref[k, x] = total[k]


def per_device(
    displacement,
    cell_scale,
    material_id,
    stiff_table,
    mass_table,
    pile_block,
    pile_owner,
    node_index,
):
    planes, ny, nz = cell_scale.shape
    rows = planes * ny
    tiles = lax.axis_size("tile")
    chips = tiles // 2
    _, block_count, width = node_index.shape
    blocks = tiles * block_count
    vmem = pl.BlockSpec(memory_space=pltpu.VMEM)
    smem = pl.BlockSpec(memory_space=pltpu.SMEM)
    hbm = pl.BlockSpec(memory_space=pltpu.HBM)
    anywhere = pl.BlockSpec(memory_space=pl.ANY)
    dma = pltpu.SemaphoreType.DMA

    def call(kernel, name, out_shape, in_specs, scratch=(), flops=10**8, moved=10**6):
        return pl.pallas_call(
            kernel,
            out_shape=out_shape,
            in_specs=in_specs,
            out_specs=jax.tree.map(lambda _: vmem, out_shape),
            scratch_shapes=list(scratch),
            compiler_params=pltpu.CompilerParams(vmem_limit_bytes=16 * 1024 * 1024),
            cost_estimate=pl.CostEstimate(flops=flops, bytes_accessed=moved, transcendentals=0),
            name=name,
        )

    def in_hbm(array):
        return pltpu.with_memory_space_constraint(array, pltpu.HBM)

    def shape(dims, kind):
        return jax.ShapeDtypeStruct(dims, kind)

    field = displacement.reshape(6, planes, ny, nz)
    nodes = node_index.transpose(1, 0, 2).reshape(blocks, width)
    owner = pile_owner.reshape(1, tiles)
    slab = (chips * 18, width)
    cut = (chips, 9, 2, width)
    pair = [(i, i ^ 1) for i in range(tiles)]
    groups = [[2 * chip + core for chip in range(chips)] for core in range(2)]

    size = (8, ny, nz)

    def exchange(payload):
        return lax.all_to_all(payload.reshape(cut), "tile", 0, 0, axis_index_groups=groups, tiled=True)

    picked, info = call(
        functools.partial(gather_kernel, tiles),
        "gather",
        (
            shape((MOST, 8, width), BF16),
            shape((3 * MOST, width), I32),
        ),
        [hbm] * 3,
        [
            pltpu.VMEM((6, rows, nz), F32),
            pltpu.VMEM((blocks, width), I32),
            pltpu.VMEM((1, tiles), I32),
            dma((3,)),
        ],
    )(in_hbm(displacement.reshape(6, rows, nz)), in_hbm(nodes), in_hbm(owner))
    payload = call(functools.partial(place_kernel, tiles), "place", shape(slab, BF16), [vmem] * 3)(
        picked, lax.ppermute(picked, "tile", pair), info
    )
    arrived = exchange(payload)

    order = pile_block.shape[-1]
    block = in_hbm(pile_block.reshape(2, order, order))
    square = (order, order)
    some = (256, order)
    to_near, to_far, imag, more = pl.pallas_call(
        ahead_kernel,
        out_shape=(shape(size, F32), shape(size, F32), shape(square, BF16), shape(some, BF16)),
        in_specs=[anywhere] + [hbm] * 4,
        out_specs=(hbm, hbm, vmem, vmem),
        scratch_shapes=[pltpu.VMEM(size, F32), pltpu.VMEM(size, F32), pltpu.VMEM(material_id.shape, I32), dma((9,))],
        compiler_params=pltpu.CompilerParams(vmem_limit_bytes=16 * 1024 * 1024),
        cost_estimate=pl.CostEstimate(flops=10**8, bytes_accessed=10**6, transcendentals=0),
        name="ahead",
    )(payload, *map(in_hbm, (field, cell_scale, material_id)), block)
    near = lax.ppermute(to_near, "tile", pair)
    next_chip = [(i, (i + 1) % tiles) for i in range(1, tiles, 2)]
    far = lax.ppermute(to_far, "tile", next_chip + [(j, i) for i, j in next_chip])
    token = call(token_kernel, "token", shape((8, width), F32), [anywhere], flops=10**11)(to_far)
    returning = call(
        pile_kernel,
        "pile",
        shape(slab, BF16),
        [vmem, vmem, vmem, hbm, vmem, anywhere],
        [pltpu.VMEM(square, BF16), dma((2,))],
    )(arrived, imag, more, block, info, token)
    landed = exchange(returning)
    soil, slot_row, at_column = call(
        functools.partial(soil_kernel, tiles),
        "soil",
        (shape(field.shape, F32), shape((MOST, width), I32), shape((nz, MOST * width), BF16)),
        [anywhere] + [hbm] * 6 + [smem] * 2,
        [
            pltpu.VMEM(field.shape, F32),
            pltpu.VMEM(cell_scale.shape, F32),
            pltpu.VMEM(cell_scale.shape, I32),
            pltpu.VMEM(size, F32),
            pltpu.VMEM(size, F32),
            pltpu.VMEM((blocks, width), I32),
            dma((6,)),
        ],
        flops=10**11,
        moved=10**7,
    )(returning, *map(in_hbm, (field, cell_scale, material_id, near, far, nodes)), stiff_table, mass_table)
    slots = shape((MOST, 8, width), BF16)
    own, twin = call(functools.partial(choose_kernel, tiles), "choose", (slots, slots), [vmem] * 2 + [anywhere])(
        landed.reshape(slab), info, soil
    )
    twin = lax.ppermute(twin, "tile", pair)
    result = call(
        scatter_kernel,
        "scatter",
        shape((6, rows, nz), F32),
        [vmem] * 5,
        [pltpu.VMEM((6 * rows, MOST * width), BF16)],
    )(soil.reshape(6, rows, nz), own, twin, slot_row, at_column)
    return result.reshape(displacement.shape)


def solution(mesh):
    placed = (
        P(None, None, ("freq", "tile"), None, None),
        P("tile", None, None),
        P("tile", None, None),
        P(None, "freq"),
        P(None, "freq"),
        P(("freq", "tile"), None, None, None),
        P("freq"),
        P(),
    )
    return jax.shard_map(
        per_device,
        mesh=mesh,
        in_specs=placed,
        out_specs=P(None, None, ("freq", "tile"), None, None),
        check_vma=False,
    )
```

```python
import functools

import jax
import jax.numpy as jnp
from jax import lax
from jax.experimental import pallas as pl
from jax.experimental.pallas import tpu as pltpu
from jax.sharding import PartitionSpec as P

MOST = 8
F32 = jnp.float32
BF16 = jnp.bfloat16
I32 = jnp.int32
NT = (((1,), (1,)), ((), ()))


def iota(shape, axis):
    return lax.broadcasted_iota(I32, shape, axis)


def onehot(mask):
    return jnp.where(mask, 1.0, 0.0).astype(BF16)


def dot(left, right):
    return jnp.dot(left, right, preferred_element_type=F32)


def dot_nt(left, right):
    return lax.dot_general(left, right, NT, preferred_element_type=F32)


def slots_of(nodes, me, cells, columns):
    blocks, width = nodes.shape
    local = nodes - me * cells
    inside = (local >= 0) & (local < cells)
    shift = columns.bit_length() - 1
    row1 = jnp.where(inside, (local >> shift) + 1, 0).astype(F32).astype(BF16)
    column = jnp.where(inside, local & (columns - 1), 0).astype(F32).astype(BF16)
    first = onehot(iota((MOST, width), 1) == 0)
    onto = dot_nt(first, onehot(inside))
    upper = onehot(iota((blocks, blocks), 0) < iota((blocks, blocks), 1))
    rank = dot(onto.astype(BF16), upper)
    slot = (onto > 0.5) & (rank == iota((MOST, blocks), 0).astype(F32))
    chosen = onehot(slot)
    return slot, dot(chosen, row1).astype(I32) - 1, dot(chosen, column).astype(I32)


def gather_kernel(
    tiles,
    displacement_hbm,
    nodes_hbm,
    owner_hbm,
    picked_ref,
    displacement,
    node_buffer,
    owner_buffer,
    semaphores,
):
    me = lax.axis_index("tile")
    copies = [
        pltpu.make_async_copy(source, target, semaphores.at[i])
        for i, (source, target) in enumerate(
            ((nodes_hbm, node_buffer), (owner_hbm, owner_buffer), (displacement_hbm, displacement))
        )
    ]
    for copy in copies:
        copy.start()
    copies[0].wait()
    copies[1].wait()
    components, rows, columns = displacement.shape
    blocks, width = node_buffer.shape
    block_count = blocks // tiles
    nodes = node_buffer[...]
    owner = owner_buffer[...]
    cells = rows * columns
    slot, slot_row, slot_column = slots_of(nodes, me, cells, columns)
    target = jnp.concatenate([owner + (b * tiles + 1) for b in range(block_count)], axis=1)
    target = jnp.sum(jnp.where(slot, target.astype(F32), 0.0), axis=1, keepdims=True)
    target = jnp.broadcast_to(target, (MOST, width))
    copies[2].wait()
    field = displacement[...].reshape(components * rows, columns).astype(BF16)
    empty = jnp.zeros((7 - components, width), F32)
    for pair in range(MOST // 2):
        at_column = jnp.concatenate(
            [
                onehot(iota((columns, width), 0) == slot_column[s : s + 1, :])
                for s in (2 * pair, 2 * pair + 1)
            ],
            axis=1,
        )
        taken = dot(field, at_column)
        for i in range(2):
            s = 2 * pair + i
            at_row = iota((rows, width), 0) == slot_row[s : s + 1, :]
            found = []
            for r in range(components):
                k = component(r)
                one = taken[k * rows : (k + 1) * rows, i * width : (i + 1) * width]
                found.append(jnp.sum(jnp.where(at_row, one, 0.0), axis=0, keepdims=True))
            picked_ref[s] = jnp.concatenate(found + [target[s : s + 1, :], empty], axis=0).astype(BF16)


def component(row):
    return (row & 1) * 3 + (row >> 1)


def payload_rows(targets, row, tiles, core):
    owner = targets & (tiles - 1)
    block = targets >> (tiles.bit_length() - 1)
    code = (owner >> 1) * 18 + block * 2 + (row >> 1) * 6 + (row & 1)
    return jnp.where((targets >= 0) & ((owner & 1) == core) & (row < 6), code, -1)


def place_kernel(tiles, picked_ref, twin_ref, payload_ref, target_ref):
    core = lax.axis_index("tile") & 1
    rows, width = payload_ref.shape
    picked = jnp.concatenate([picked_ref[...].reshape(MOST * 8, width), twin_ref[...].reshape(MOST * 8, width)], axis=0)
    targets = jnp.concatenate([ref[s, 6:7, :].astype(F32) for ref in (picked_ref, twin_ref) for s in range(MOST)], axis=0)
    targets = targets.astype(I32) - 1
    target_ref[...] = targets
    lane = iota((2 * MOST, width), 1)
    code = payload_rows(targets, lane & 7, tiles, core)
    code = jnp.sum(jnp.where((lane >> 3) == iota((2 * MOST, width), 0), code, 0), axis=0, keepdims=True)
    place = onehot(iota((rows, width), 0) == code)
    payload_ref[...] = dot(place, picked).astype(BF16)


def pile_kernel(arrived_ref, imag_ref, more_ref, block_hbm, chip_ref, order_ref, payload_ref, real_ref, semaphores):
    rows, width = payload_ref.shape
    _, pieces, _, _ = arrived_ref.shape
    order = imag_ref.shape[0]
    ahead = more_ref.shape[0]
    ends = (ahead, 640, order)
    copies = []
    for i, (start, stop) in enumerate(zip(ends, ends[1:])):
        copies.append(pltpu.make_async_copy(block_hbm.at[0, start:stop], real_ref.at[start:stop], semaphores.at[i]))
        copies[i].start()
    vector = jnp.sum(arrived_ref[...].astype(F32), axis=0)
    vector = jnp.concatenate([vector[k] for k in range(pieces)], axis=1).astype(BF16)
    by_imag = dot_nt(vector, imag_ref[...])
    by_real = [dot_nt(vector, more_ref[...])]
    for i, (start, stop) in enumerate(zip(ends, ends[1:])):
        copies[i].wait()
        by_real.append(dot_nt(vector, real_ref[start:stop, :]))
    by_real = jnp.concatenate(by_real, axis=1)
    real = by_real[0:1] - by_imag[1:2]
    imag = by_real[1:2] + by_imag[0:1]
    traction = [part[:, k * width : (k + 1) * width] for k in range(pieces) for part in (real, imag)]
    traction = jnp.concatenate(traction + [jnp.zeros((width - 2 * pieces, width), F32)], axis=0).astype(BF16)
    lane = iota((1, width), 1)
    block = (lane >> 1) % 3
    chip = chip_ref[0:1, :]
    for b in (1, 2):
        chip = jnp.where(block == b, chip_ref[b : b + 1, :], chip)
    code = jnp.where(lane < 2 * pieces, chip * (2 * pieces) + lane, -1)
    place = onehot(iota((rows, width), 0) == code)
    payload_ref[...] = dot(place, traction).astype(BF16)


def choose_kernel(tiles, landed_ref, target_ref, order_ref, own_ref, twin_ref):
    core = lax.axis_index("tile") & 1
    slab, width = landed_ref.shape
    count = 2 * MOST
    shape = (count, 8, slab)
    targets = target_ref[:, 0:1].reshape(count, 1, 1)
    code = payload_rows(targets, iota((count, 8, 1), 1), tiles, core)
    take = onehot(iota(shape, 2) == code).reshape(count * 8, slab)
    chosen = dot(take, landed_ref[...]).astype(BF16).reshape(2, MOST, 8, width)
    own_ref[...] = chosen[0]
    twin_ref[...] = chosen[1]


def scatter_kernel(soil_ref, own_ref, twin_ref, at_row_ref, at_column_ref, result_hbm, result, semaphores):
    components, rows, columns = soil_ref.shape
    pieces = [own_ref[s].astype(F32) + twin_ref[s].astype(F32) for s in range(MOST)]
    pieces = jnp.concatenate(pieces, axis=1)
    at_row = at_row_ref[...]
    half = components // 2
    copies = []
    for i in range(2):
        spread = []
        for k in range(i * half, (i + 1) * half):
            row = (k % half) * 2 + i
            spread.append(jnp.broadcast_to(pieces[row : row + 1, :], at_row.shape).astype(BF16) * at_row)
        added = dot_nt(jnp.concatenate(spread, axis=0), at_column_ref[...])
        part = slice(i * half, (i + 1) * half)
        result[part] = soil_ref[part] + added.reshape(half, rows, columns)
        copies.append(pltpu.make_async_copy(result.at[part], result_hbm.at[part], semaphores.at[i]))
        copies[i].start()
    for copy in copies:
        copy.wait()


def ahead_kernel(
    order_ref,
    displacement_hbm,
    scale_hbm,
    kind_hbm,
    block_hbm,
    nodes_hbm,
    owner_hbm,
    near_hbm,
    far_hbm,
    imag_ref,
    more_ref,
    chip_ref,
    near,
    far,
    kind,
    node_buffer,
    owner_buffer,
    semaphores,
):
    planes = scale_hbm.shape[0]
    odd = lax.axis_index("tile") & 1
    sides = ((near, near_hbm, (1 - odd) * (planes - 1)), (far, far_hbm, odd * (planes - 1)))
    pairs = [(kind_hbm, kind)]
    for plane, _, x in sides:
        pairs += [(displacement_hbm.at[:, x], plane.at[0:6]), (scale_hbm.at[x], plane.at[6])]
    pairs += [(block_hbm.at[1], imag_ref), (block_hbm.at[0, 0 : more_ref.shape[0]], more_ref)]
    pairs += [(nodes_hbm, node_buffer), (owner_hbm, owner_buffer)]
    copies = [pltpu.make_async_copy(*pair, semaphores.at[i]) for i, pair in enumerate(pairs)]
    for copy in copies:
        copy.start()
    copies[0].wait()
    for plane, _, x in sides:
        plane[7] = kind[x].astype(F32)
    sends = []
    for i, (plane, target, _) in enumerate(sides):
        copies[2 * i + 1].wait()
        copies[2 * i + 2].wait()
        sends.append(pltpu.make_async_copy(plane, target, semaphores.at[9 + i]))
        sends[i].start()
    copies[7].wait()
    copies[8].wait()
    blocks, width = node_buffer.shape
    tiles = owner_buffer.shape[1]
    cells = planes * displacement_hbm.shape[2] * displacement_hbm.shape[3]
    first = onehot(iota((MOST, width), 1) == 0)
    tile_of = jnp.floor(((node_buffer[...] >> 13).astype(F32) + 0.5) * (1.0 / (cells >> 13)))
    tile_row = dot_nt(first, tile_of.astype(BF16))[0:1, :]
    mine = owner_buffer[...] == lax.axis_index("tile")
    for b in range(blocks // tiles):
        own = jnp.sum(jnp.where(mine, tile_row[:, b * tiles : (b + 1) * tiles], 0.0), axis=1, keepdims=True)
        chip_ref[b : b + 1, :] = jnp.broadcast_to(own.astype(I32) >> 1, (1, width))
    for copy in copies[5:7] + sends:
        copy.wait()


def token_kernel(order_ref, token_ref):
    token_ref[...] = jnp.zeros(token_ref.shape, F32)


def lookup(table_ref, row, kind):
    bits = [(kind & (1 << k)) != 0 for k in range(4)]
    level = [table_ref[row, k] for k in range(16)]
    for bit in bits:
        level = [jnp.where(bit, level[2 * k + 1], level[2 * k]) for k in range(len(level) // 2)]
    return level[0]


def half_stiffness(table_ref, kind, scale):
    return [0.5 * (lookup(table_ref, i, kind) * scale) for i in range(2)]


def flux(face, near, far):
    strain = [near[k] - far[k] for k in range(6)]
    real = [face[0] * strain[c] - face[1] * strain[3 + c] for c in range(3)]
    imag = [face[0] * strain[3 + c] + face[1] * strain[c] for c in range(3)]
    return real + imag


def soil_kernel(
    tiles,
    order_ref,
    displacement_hbm,
    scale_hbm,
    kind_hbm,
    near_hbm,
    far_hbm,
    nodes_hbm,
    stiff_ref,
    mass_ref,
    soil_ref,
    at_row_ref,
    at_column_ref,
    displacement_ref,
    scale_ref,
    kind_ref,
    near_ref,
    far_ref,
    node_buffer,
    semaphores,
):
    sources = (nodes_hbm, kind_hbm, scale_hbm, displacement_hbm, near_hbm, far_hbm)
    targets = (node_buffer, kind_ref, scale_ref, displacement_ref, near_ref, far_ref)
    copies = [pltpu.make_async_copy(*two, semaphores.at[i]) for i, two in enumerate(zip(sources, targets))]
    for copy in copies:
        copy.start()
    _, planes, ny, nz = displacement_ref.shape
    shape = (ny, nz)
    tile = lax.axis_index("tile")
    odd = tile & 1
    even = odd == 0
    copies[0].wait()
    width = node_buffer.shape[1]
    _, slot_row, slot_column = slots_of(node_buffer[...], tile, planes * ny * nz, nz)
    for s in range(MOST):
        lanes = slice(s * width, (s + 1) * width)
        at_row_ref[:, lanes] = onehot(iota((planes * ny, width), 0) == slot_row[s : s + 1, :])
        at_column_ref[:, lanes] = onehot(iota((nz, width), 0) == slot_column[s : s + 1, :])
    for copy in copies[1:]:
        copy.wait()

    @pl.when((tile == 0) | (tile == tiles - 1))
    def _():
        far_ref[...] = jnp.zeros(far_ref.shape, F32)

    at_y, at_z = iota(shape, 0), iota(shape, 1)
    y_last, z_last = at_y == ny - 1, at_z == nz - 1
    edges = (
        jnp.where(at_y == 0, 0.5, 0.0)
        + jnp.where(y_last, 0.5, 0.0)
        + jnp.where(at_z == 0, 0.5, 0.0)
        + jnp.where(z_last, 0.5, 0.0)
    )
    half = [half_stiffness(stiff_ref, kind_ref[x], scale_ref[x]) for x in range(planes)]
    fields = [[displacement_ref[k, x] for k in range(6)] for x in range(planes)]

    def outside(first, second, flag):
        return [jnp.where(flag, first[k], second[k]) for k in range(6)], [
            jnp.where(flag, a, b)
            for a, b in zip(*(half_stiffness(stiff_ref, ref[7].astype(I32), ref[6]) for ref in (first, second)))
        ]

    before, before_half = outside(far_ref, near_ref, even)
    after, after_half = outside(near_ref, far_ref, even)
    fields = [before] + fields + [after]
    half = [before_half] + half + [after_half]

    def x_flux(x):
        return flux([half[x][i] + half[x + 1][i] for i in range(2)], fields[x], fields[x + 1])

    before = x_flux(0)
    for x in range(planes):
        u, own = fields[x + 1], half[x + 1]
        diagonal = [lookup(mass_ref, i, kind_ref[x]) + 2.0 * edges * own[i] for i in range(2)]
        total = [diagonal[0] * u[c] - diagonal[1] * u[3 + c] for c in range(3)]
        total += [diagonal[0] * u[3 + c] + diagonal[1] * u[c] for c in range(3)]
        beyond = x_flux(x + 1)
        total = [total[k] + beyond[k] - before[k] for k in range(6)]
        before = beyond
        for axis, last in ((0, y_last), (1, z_last)):
            size = shape[axis]
            face = [jnp.where(last, 0.0, own[i] + pltpu.roll(own[i], size - 1, axis)) for i in range(2)]
            next_to = [pltpu.roll(u[k], size - 1, axis) for k in range(6)]
            along = flux(face, u, next_to)
            total = [total[k] + along[k] - pltpu.roll(along[k], 1, axis) for k in range(6)]
        for k in range(6):
            soil_ref[k, x] = total[k]


def per_device(
    displacement,
    cell_scale,
    material_id,
    stiff_table,
    mass_table,
    pile_block,
    pile_owner,
    node_index,
):
    planes, ny, nz = cell_scale.shape
    rows = planes * ny
    tiles = lax.axis_size("tile")
    chips = tiles // 2
    _, block_count, width = node_index.shape
    blocks = tiles * block_count
    vmem = pl.BlockSpec(memory_space=pltpu.VMEM)
    smem = pl.BlockSpec(memory_space=pltpu.SMEM)
    hbm = pl.BlockSpec(memory_space=pltpu.HBM)
    anywhere = pl.BlockSpec(memory_space=pl.ANY)
    dma = pltpu.SemaphoreType.DMA

    def call(kernel, name, out_shape, in_specs, scratch=(), flops=10**8, moved=10**6):
        return pl.pallas_call(
            kernel,
            out_shape=out_shape,
            in_specs=in_specs,
            out_specs=jax.tree.map(lambda _: vmem, out_shape),
            scratch_shapes=list(scratch),
            compiler_params=pltpu.CompilerParams(vmem_limit_bytes=16 * 1024 * 1024),
            cost_estimate=pl.CostEstimate(flops=flops, bytes_accessed=moved, transcendentals=0),
            name=name,
        )

    def in_hbm(array):
        return pltpu.with_memory_space_constraint(array, pltpu.HBM)

    def shape(dims, kind):
        return jax.ShapeDtypeStruct(dims, kind)

    field = displacement.reshape(6, planes, ny, nz)
    nodes = node_index.transpose(1, 0, 2).reshape(blocks, width)
    owner = pile_owner.reshape(1, tiles)
    slab = (chips * 18, width)
    cut = (chips, 9, 2, width)
    pair = [(i, i ^ 1) for i in range(tiles)]
    groups = [[2 * chip + core for chip in range(chips)] for core in range(2)]

    size = (8, ny, nz)

    def exchange(payload):
        return lax.all_to_all(payload.reshape(cut), "tile", 0, 0, axis_index_groups=groups, tiled=True)

    picked = call(
        functools.partial(gather_kernel, tiles),
        "gather",
        shape((MOST, 8, width), BF16),
        [hbm] * 3,
        [
            pltpu.VMEM((6, rows, nz), F32),
            pltpu.VMEM((blocks, width), I32),
            pltpu.VMEM((1, tiles), I32),
            dma((3,)),
        ],
    )(in_hbm(displacement.reshape(6, rows, nz)), in_hbm(nodes), in_hbm(owner))
    payload, targets = call(
        functools.partial(place_kernel, tiles),
        "place",
        (shape(slab, BF16), shape((2 * MOST, width), I32)),
        [vmem] * 2,
    )(picked, lax.ppermute(picked, "tile", pair))
    arrived = exchange(payload)

    order = pile_block.shape[-1]
    block = in_hbm(pile_block.reshape(2, order, order))
    square = (order, order)
    some = (256, order)
    to_near, to_far, imag, more, chip = pl.pallas_call(
        ahead_kernel,
        out_shape=(shape(size, F32), shape(size, F32), shape(square, BF16), shape(some, BF16), shape((MOST, width), I32)),
        in_specs=[anywhere] + [hbm] * 6,
        out_specs=(hbm, hbm, vmem, vmem, vmem),
        scratch_shapes=[
            pltpu.VMEM(size, F32),
            pltpu.VMEM(size, F32),
            pltpu.VMEM(material_id.shape, I32),
            pltpu.VMEM((blocks, width), I32),
            pltpu.VMEM((1, tiles), I32),
            dma((11,)),
        ],
        compiler_params=pltpu.CompilerParams(vmem_limit_bytes=16 * 1024 * 1024),
        cost_estimate=pl.CostEstimate(flops=10**8, bytes_accessed=10**6, transcendentals=0),
        name="ahead",
    )(payload, *map(in_hbm, (field, cell_scale, material_id)), block, in_hbm(nodes), in_hbm(owner))
    near = lax.ppermute(to_near, "tile", pair)
    next_chip = [(i, (i + 1) % tiles) for i in range(1, tiles, 2)]
    far = lax.ppermute(to_far, "tile", next_chip + [(j, i) for i, j in next_chip])
    token = call(token_kernel, "token", shape((8, width), F32), [anywhere], flops=10**11)(to_far)
    returning = call(
        pile_kernel,
        "pile",
        shape(slab, BF16),
        [vmem, vmem, vmem, hbm, vmem, anywhere],
        [pltpu.VMEM(square, BF16), dma((2,))],
    )(arrived, imag, more, block, chip, token)
    landed = exchange(returning)
    soil, at_row, at_column = call(
        functools.partial(soil_kernel, tiles),
        "soil",
        (shape(field.shape, F32), shape((rows, MOST * width), BF16), shape((nz, MOST * width), BF16)),
        [anywhere] + [hbm] * 6 + [smem] * 2,
        [
            pltpu.VMEM(field.shape, F32),
            pltpu.VMEM(cell_scale.shape, F32),
            pltpu.VMEM(cell_scale.shape, I32),
            pltpu.VMEM(size, F32),
            pltpu.VMEM(size, F32),
            pltpu.VMEM((blocks, width), I32),
            dma((6,)),
        ],
        flops=10**11,
        moved=10**7,
    )(returning, *map(in_hbm, (field, cell_scale, material_id, near, far, nodes)), stiff_table, mass_table)
    slots = shape((MOST, 8, width), BF16)
    own, twin = call(functools.partial(choose_kernel, tiles), "choose", (slots, slots), [vmem] * 2 + [anywhere])(
        landed.reshape(slab), targets, soil
    )
    twin = lax.ppermute(twin, "tile", pair)
    sums = (6, rows, nz)
    result = pl.pallas_call(
        scatter_kernel,
        out_shape=shape(sums, F32),
        in_specs=[vmem] * 5,
        out_specs=hbm,
        scratch_shapes=[pltpu.VMEM(sums, F32), dma((2,))],
        compiler_params=pltpu.CompilerParams(vmem_limit_bytes=16 * 1024 * 1024),
        cost_estimate=pl.CostEstimate(flops=10**8, bytes_accessed=10**6, transcendentals=0),
        name="scatter",
    )(soil.reshape(sums), own, twin, at_row, at_column)
    return result.reshape(displacement.shape)


def solution(mesh):
    placed = (
        P(None, None, ("freq", "tile"), None, None),
        P("tile", None, None),
        P("tile", None, None),
        P(None, "freq"),
        P(None, "freq"),
        P(("freq", "tile"), None, None, None),
        P("freq"),
        P(),
    )
    return jax.shard_map(
        per_device,
        mesh=mesh,
        in_specs=placed,
        out_specs=P(None, None, ("freq", "tile"), None, None),
        check_vma=False,
    )
```

```python
import functools

import jax
import jax.numpy as jnp
from jax import lax
from jax.experimental import pallas as pl
from jax.experimental.pallas import tpu as pltpu
from jax.sharding import PartitionSpec as P

MOST = 8
F32 = jnp.float32
BF16 = jnp.bfloat16
I32 = jnp.int32
NT = (((1,), (1,)), ((), ()))


def iota(shape, axis):
    return lax.broadcasted_iota(I32, shape, axis)


def onehot(mask):
    return jnp.where(mask, 1.0, 0.0).astype(BF16)


def dot(left, right):
    return jnp.dot(left, right, preferred_element_type=F32)


def dot_nt(left, right):
    return lax.dot_general(left, right, NT, preferred_element_type=F32)


def slots_of(nodes, me, cells, columns):
    blocks, width = nodes.shape
    local = nodes - me * cells
    inside = (local >= 0) & (local < cells)
    shift = columns.bit_length() - 1
    row1 = jnp.where(inside, (local >> shift) + 1, 0).astype(F32).astype(BF16)
    column = jnp.where(inside, local & (columns - 1), 0).astype(F32).astype(BF16)
    first = onehot(iota((MOST, width), 1) == 0)
    onto = dot_nt(first, onehot(inside))
    upper = onehot(iota((blocks, blocks), 0) < iota((blocks, blocks), 1))
    rank = dot(onto.astype(BF16), upper)
    slot = (onto > 0.5) & (rank == iota((MOST, blocks), 0).astype(F32))
    places = dot(onehot(slot), jnp.concatenate([row1, column], axis=1)).astype(I32)
    return slot, places[:, :width] - 1, places[:, width:]


def gather_kernel(
    tiles,
    displacement_hbm,
    nodes_hbm,
    owner_hbm,
    picked_ref,
    displacement,
    node_buffer,
    owner_buffer,
    semaphores,
):
    me = lax.axis_index("tile")
    copies = [
        pltpu.make_async_copy(source, target, semaphores.at[i])
        for i, (source, target) in enumerate(
            ((nodes_hbm, node_buffer), (owner_hbm, owner_buffer), (displacement_hbm, displacement))
        )
    ]
    for copy in copies:
        copy.start()
    copies[0].wait()
    copies[1].wait()
    components, rows, columns = displacement.shape
    blocks, width = node_buffer.shape
    block_count = blocks // tiles
    nodes = node_buffer[...]
    owner = owner_buffer[...]
    cells = rows * columns
    slot, slot_row, slot_column = slots_of(nodes, me, cells, columns)
    target = jnp.concatenate([owner + (b * tiles + 1) for b in range(block_count)], axis=1)
    target = jnp.sum(jnp.where(slot, target.astype(F32), 0.0), axis=1, keepdims=True)
    target = jnp.broadcast_to(target, (MOST, width))
    copies[2].wait()
    field = displacement[...].reshape(components * rows, columns).astype(BF16)
    empty = jnp.zeros((7 - components, width), F32)
    for pair in range(MOST // 2):
        at_column = jnp.concatenate(
            [
                onehot(iota((columns, width), 0) == slot_column[s : s + 1, :])
                for s in (2 * pair, 2 * pair + 1)
            ],
            axis=1,
        )
        taken = dot(field, at_column)
        for i in range(2):
            s = 2 * pair + i
            at_row = iota((rows, width), 0) == slot_row[s : s + 1, :]
            found = []
            for r in range(components):
                k = component(r)
                one = taken[k * rows : (k + 1) * rows, i * width : (i + 1) * width]
                found.append(jnp.sum(jnp.where(at_row, one, 0.0), axis=0, keepdims=True))
            picked_ref[s] = jnp.concatenate(found + [target[s : s + 1, :], empty], axis=0)


def component(row):
    return (row & 1) * 3 + (row >> 1)


def payload_rows(targets, row, tiles, core):
    owner = targets & (tiles - 1)
    block = targets >> (tiles.bit_length() - 1)
    code = (owner >> 1) * 18 + block * 2 + (row >> 1) * 6 + (row & 1)
    return jnp.where((targets >= 0) & ((owner & 1) == core) & (row < 6), code, -1)


def place_kernel(tiles, picked_ref, twin_ref, payload_ref, target_ref):
    core = lax.axis_index("tile") & 1
    rows, width = payload_ref.shape
    picked = jnp.concatenate([picked_ref[...].reshape(MOST * 8, width), twin_ref[...].reshape(MOST * 8, width)], axis=0)
    targets = jnp.concatenate([ref[s, 6:7, :] for ref in (picked_ref, twin_ref) for s in range(MOST)], axis=0)
    targets = targets.astype(I32) - 1
    target_ref[...] = targets
    lane = iota((2 * MOST, width), 1)
    code = payload_rows(targets, lane & 7, tiles, core)
    code = jnp.sum(jnp.where((lane >> 3) == iota((2 * MOST, width), 0), code, 0), axis=0, keepdims=True)
    place = onehot(iota((rows, width), 0) == code)
    payload_ref[...] = dot(place, picked.astype(BF16)).astype(BF16)


def pile_kernel(arrived_ref, imag_ref, more_ref, block_hbm, chip_ref, order_ref, payload_ref, real_ref, semaphores):
    rows, width = payload_ref.shape
    _, pieces, _, _ = arrived_ref.shape
    order = imag_ref.shape[0]
    ahead = more_ref.shape[0]
    ends = (ahead, 640, order)
    copies = []
    for i, (start, stop) in enumerate(zip(ends, ends[1:])):
        copies.append(pltpu.make_async_copy(block_hbm.at[0, start:stop], real_ref.at[start:stop], semaphores.at[i]))
        copies[i].start()
    vector = jnp.sum(arrived_ref[...].astype(F32), axis=0)
    vector = jnp.concatenate([vector[k] for k in range(pieces)], axis=1).astype(BF16)
    by_imag = dot_nt(vector, imag_ref[...])
    by_real = [dot_nt(vector, more_ref[...])]
    for i, (start, stop) in enumerate(zip(ends, ends[1:])):
        copies[i].wait()
        by_real.append(dot_nt(vector, real_ref[start:stop, :]))
    by_real = jnp.concatenate(by_real, axis=1)
    real = by_real[0:1] - by_imag[1:2]
    imag = by_real[1:2] + by_imag[0:1]
    traction = [part[:, k * width : (k + 1) * width] for k in range(pieces) for part in (real, imag)]
    traction = jnp.concatenate(traction + [jnp.zeros((width - 2 * pieces, width), F32)], axis=0).astype(BF16)
    lane = iota((1, width), 1)
    block = (lane >> 1) % 3
    chip = chip_ref[0:1, :]
    for b in (1, 2):
        chip = jnp.where(block == b, chip_ref[b : b + 1, :], chip)
    code = jnp.where(lane < 2 * pieces, chip * (2 * pieces) + lane, -1)
    place = onehot(iota((rows, width), 0) == code)
    payload_ref[...] = dot(place, traction).astype(BF16)


def choose_kernel(tiles, landed_ref, target_ref, order_ref, own_ref, twin_ref):
    core = lax.axis_index("tile") & 1
    slab, width = landed_ref.shape
    count = 2 * MOST
    shape = (count, 8, slab)
    targets = target_ref[:, 0:1].reshape(count, 1, 1)
    code = payload_rows(targets, iota((count, 8, 1), 1), tiles, core)
    take = onehot(iota(shape, 2) == code).reshape(count * 8, slab)
    chosen = dot(take, landed_ref[...]).reshape(2, MOST, 8, width)
    own_ref[...] = chosen[0]
    twin_ref[...] = chosen[1]


def scatter_kernel(soil_ref, own_ref, twin_ref, at_row_ref, at_column_ref, result_hbm, result, semaphores):
    components, rows, columns = soil_ref.shape
    pieces = [own_ref[s] + twin_ref[s] for s in range(MOST)]
    pieces = jnp.concatenate(pieces, axis=1)
    at_row = at_row_ref[...]
    half = components // 2
    copies = []
    for i in range(2):
        spread = []
        for k in range(i * half, (i + 1) * half):
            row = (k % half) * 2 + i
            spread.append(jnp.broadcast_to(pieces[row : row + 1, :], at_row.shape).astype(BF16) * at_row)
        added = dot_nt(jnp.concatenate(spread, axis=0), at_column_ref[...])
        part = slice(i * half, (i + 1) * half)
        result[part] = soil_ref[part] + added.reshape(half, rows, columns)
        copies.append(pltpu.make_async_copy(result.at[part], result_hbm.at[part], semaphores.at[i]))
        copies[i].start()
    for copy in copies:
        copy.wait()


def ahead_kernel(
    order_ref,
    displacement_hbm,
    scale_hbm,
    kind_hbm,
    block_hbm,
    nodes_hbm,
    owner_hbm,
    near_hbm,
    far_hbm,
    imag_ref,
    more_ref,
    chip_ref,
    near,
    far,
    kind,
    node_buffer,
    owner_buffer,
    semaphores,
):
    planes = scale_hbm.shape[0]
    odd = lax.axis_index("tile") & 1
    sides = ((near, near_hbm, (1 - odd) * (planes - 1)), (far, far_hbm, odd * (planes - 1)))
    pairs = [(kind_hbm, kind)]
    for plane, _, x in sides:
        pairs += [(displacement_hbm.at[:, x], plane.at[0:6]), (scale_hbm.at[x], plane.at[6])]
    pairs += [(block_hbm.at[1], imag_ref), (block_hbm.at[0, 0 : more_ref.shape[0]], more_ref)]
    pairs += [(nodes_hbm, node_buffer), (owner_hbm, owner_buffer)]
    copies = [pltpu.make_async_copy(*pair, semaphores.at[i]) for i, pair in enumerate(pairs)]
    for copy in copies:
        copy.start()
    copies[0].wait()
    for plane, _, x in sides:
        plane[7] = kind[x].astype(F32)
    sends = []
    for i, (plane, target, _) in enumerate(sides):
        copies[2 * i + 1].wait()
        copies[2 * i + 2].wait()
        sends.append(pltpu.make_async_copy(plane, target, semaphores.at[9 + i]))
        sends[i].start()
    copies[7].wait()
    copies[8].wait()
    blocks, width = node_buffer.shape
    tiles = owner_buffer.shape[1]
    cells = planes * displacement_hbm.shape[2] * displacement_hbm.shape[3]
    first = onehot(iota((MOST, width), 1) == 0)
    tile_of = jnp.floor(((node_buffer[...] >> 13).astype(F32) + 0.5) * (1.0 / (cells >> 13)))
    tile_row = dot_nt(first, tile_of.astype(BF16))[0:1, :]
    mine = owner_buffer[...] == lax.axis_index("tile")
    for b in range(blocks // tiles):
        own = jnp.sum(jnp.where(mine, tile_row[:, b * tiles : (b + 1) * tiles], 0.0), axis=1, keepdims=True)
        chip_ref[b : b + 1, :] = jnp.broadcast_to(own.astype(I32) >> 1, (1, width))
    for copy in copies[5:7] + sends:
        copy.wait()


def token_kernel(order_ref, token_ref):
    token_ref[...] = jnp.zeros(token_ref.shape, F32)


def lookup(table_ref, row, kind):
    bits = [(kind & (1 << k)) != 0 for k in range(4)]
    level = [table_ref[row, k] for k in range(16)]
    for bit in bits:
        level = [jnp.where(bit, level[2 * k + 1], level[2 * k]) for k in range(len(level) // 2)]
    return level[0]


def half_stiffness(table_ref, kind, scale):
    return [0.5 * (lookup(table_ref, i, kind) * scale) for i in range(2)]


def flux(face, near, far):
    strain = [near[k] - far[k] for k in range(6)]
    real = [face[0] * strain[c] - face[1] * strain[3 + c] for c in range(3)]
    imag = [face[0] * strain[3 + c] + face[1] * strain[c] for c in range(3)]
    return real + imag


def soil_kernel(
    tiles,
    order_ref,
    displacement_hbm,
    scale_hbm,
    kind_hbm,
    near_hbm,
    far_hbm,
    nodes_hbm,
    stiff_ref,
    mass_ref,
    soil_ref,
    at_row_ref,
    at_column_ref,
    displacement_ref,
    scale_ref,
    kind_ref,
    near_ref,
    far_ref,
    node_buffer,
    semaphores,
):
    sources = (nodes_hbm, kind_hbm, scale_hbm, displacement_hbm, near_hbm, far_hbm)
    targets = (node_buffer, kind_ref, scale_ref, displacement_ref, near_ref, far_ref)
    copies = [pltpu.make_async_copy(*two, semaphores.at[i]) for i, two in enumerate(zip(sources, targets))]
    for copy in copies:
        copy.start()
    _, planes, ny, nz = displacement_ref.shape
    shape = (ny, nz)
    tile = lax.axis_index("tile")
    odd = tile & 1
    even = odd == 0
    copies[0].wait()
    width = node_buffer.shape[1]
    _, slot_row, slot_column = slots_of(node_buffer[...], tile, planes * ny * nz, nz)
    for s in range(MOST):
        lanes = slice(s * width, (s + 1) * width)
        at_row_ref[:, lanes] = onehot(iota((planes * ny, width), 0) == slot_row[s : s + 1, :])
        at_column_ref[:, lanes] = onehot(iota((nz, width), 0) == slot_column[s : s + 1, :])
    for copy in copies[1:]:
        copy.wait()

    @pl.when((tile == 0) | (tile == tiles - 1))
    def _():
        far_ref[...] = jnp.zeros(far_ref.shape, F32)

    at_y, at_z = iota(shape, 0), iota(shape, 1)
    y_last, z_last = at_y == ny - 1, at_z == nz - 1
    edges = (
        jnp.where(at_y == 0, 0.5, 0.0)
        + jnp.where(y_last, 0.5, 0.0)
        + jnp.where(at_z == 0, 0.5, 0.0)
        + jnp.where(z_last, 0.5, 0.0)
    )
    half = [half_stiffness(stiff_ref, kind_ref[x], scale_ref[x]) for x in range(planes)]
    fields = [[displacement_ref[k, x] for k in range(6)] for x in range(planes)]

    def outside(first, second, flag):
        return [jnp.where(flag, first[k], second[k]) for k in range(6)], [
            jnp.where(flag, a, b)
            for a, b in zip(*(half_stiffness(stiff_ref, ref[7].astype(I32), ref[6]) for ref in (first, second)))
        ]

    before, before_half = outside(far_ref, near_ref, even)
    after, after_half = outside(near_ref, far_ref, even)
    fields = [before] + fields + [after]
    half = [before_half] + half + [after_half]

    def x_flux(x):
        return flux([half[x][i] + half[x + 1][i] for i in range(2)], fields[x], fields[x + 1])

    before = x_flux(0)
    for x in range(planes):
        u, own = fields[x + 1], half[x + 1]
        diagonal = [lookup(mass_ref, i, kind_ref[x]) + 2.0 * edges * own[i] for i in range(2)]
        total = [diagonal[0] * u[c] - diagonal[1] * u[3 + c] for c in range(3)]
        total += [diagonal[0] * u[3 + c] + diagonal[1] * u[c] for c in range(3)]
        beyond = x_flux(x + 1)
        total = [total[k] + beyond[k] - before[k] for k in range(6)]
        before = beyond
        for axis, last in ((0, y_last), (1, z_last)):
            size = shape[axis]
            face = [jnp.where(last, 0.0, own[i] + pltpu.roll(own[i], size - 1, axis)) for i in range(2)]
            next_to = [pltpu.roll(u[k], size - 1, axis) for k in range(6)]
            along = flux(face, u, next_to)
            total = [total[k] + along[k] - pltpu.roll(along[k], 1, axis) for k in range(6)]
        for k in range(6):
            soil_ref[k, x] = total[k]


def per_device(
    displacement,
    cell_scale,
    material_id,
    stiff_table,
    mass_table,
    pile_block,
    pile_owner,
    node_index,
):
    planes, ny, nz = cell_scale.shape
    rows = planes * ny
    tiles = lax.axis_size("tile")
    chips = tiles // 2
    _, block_count, width = node_index.shape
    blocks = tiles * block_count
    vmem = pl.BlockSpec(memory_space=pltpu.VMEM)
    smem = pl.BlockSpec(memory_space=pltpu.SMEM)
    hbm = pl.BlockSpec(memory_space=pltpu.HBM)
    anywhere = pl.BlockSpec(memory_space=pl.ANY)
    dma = pltpu.SemaphoreType.DMA

    def call(kernel, name, out_shape, in_specs, scratch=(), flops=10**8, moved=10**6):
        return pl.pallas_call(
            kernel,
            out_shape=out_shape,
            in_specs=in_specs,
            out_specs=jax.tree.map(lambda _: vmem, out_shape),
            scratch_shapes=list(scratch),
            compiler_params=pltpu.CompilerParams(vmem_limit_bytes=16 * 1024 * 1024),
            cost_estimate=pl.CostEstimate(flops=flops, bytes_accessed=moved, transcendentals=0),
            name=name,
        )

    def in_hbm(array):
        return pltpu.with_memory_space_constraint(array, pltpu.HBM)

    def shape(dims, kind):
        return jax.ShapeDtypeStruct(dims, kind)

    field = displacement.reshape(6, planes, ny, nz)
    nodes = node_index.transpose(1, 0, 2).reshape(blocks, width)
    owner = pile_owner.reshape(1, tiles)
    slab = (chips * 18, width)
    cut = (chips, 9, 2, width)
    pair = [(i, i ^ 1) for i in range(tiles)]
    groups = [[2 * chip + core for chip in range(chips)] for core in range(2)]

    size = (8, ny, nz)

    def exchange(payload):
        return lax.all_to_all(payload.reshape(cut), "tile", 0, 0, axis_index_groups=groups, tiled=True)

    picked = call(
        functools.partial(gather_kernel, tiles),
        "gather",
        shape((MOST, 8, width), F32),
        [hbm] * 3,
        [
            pltpu.VMEM((6, rows, nz), F32),
            pltpu.VMEM((blocks, width), I32),
            pltpu.VMEM((1, tiles), I32),
            dma((3,)),
        ],
    )(in_hbm(displacement.reshape(6, rows, nz)), in_hbm(nodes), in_hbm(owner))
    payload, targets = call(
        functools.partial(place_kernel, tiles),
        "place",
        (shape(slab, BF16), shape((2 * MOST, width), I32)),
        [vmem] * 2,
    )(picked, lax.ppermute(picked, "tile", pair))
    arrived = exchange(payload)

    order = pile_block.shape[-1]
    block = in_hbm(pile_block.reshape(2, order, order))
    square = (order, order)
    some = (256, order)
    to_near, to_far, imag, more, chip = pl.pallas_call(
        ahead_kernel,
        out_shape=(shape(size, F32), shape(size, F32), shape(square, BF16), shape(some, BF16), shape((MOST, width), I32)),
        in_specs=[anywhere] + [hbm] * 6,
        out_specs=(hbm, hbm, vmem, vmem, vmem),
        scratch_shapes=[
            pltpu.VMEM(size, F32),
            pltpu.VMEM(size, F32),
            pltpu.VMEM(material_id.shape, I32),
            pltpu.VMEM((blocks, width), I32),
            pltpu.VMEM((1, tiles), I32),
            dma((11,)),
        ],
        compiler_params=pltpu.CompilerParams(vmem_limit_bytes=16 * 1024 * 1024),
        cost_estimate=pl.CostEstimate(flops=10**8, bytes_accessed=10**6, transcendentals=0),
        name="ahead",
    )(payload, *map(in_hbm, (field, cell_scale, material_id)), block, in_hbm(nodes), in_hbm(owner))
    near = lax.ppermute(to_near, "tile", pair)
    next_chip = [(i, (i + 1) % tiles) for i in range(1, tiles, 2)]
    far = lax.ppermute(to_far, "tile", next_chip + [(j, i) for i, j in next_chip])
    token = call(token_kernel, "token", shape((8, width), F32), [anywhere], flops=10**11)(to_far)
    returning = call(
        pile_kernel,
        "pile",
        shape(slab, BF16),
        [vmem, vmem, vmem, hbm, vmem, anywhere],
        [pltpu.VMEM(square, BF16), dma((2,))],
    )(arrived, imag, more, block, chip, token)
    landed = exchange(returning)
    soil, at_row, at_column = call(
        functools.partial(soil_kernel, tiles),
        "soil",
        (shape(field.shape, F32), shape((rows, MOST * width), BF16), shape((nz, MOST * width), BF16)),
        [anywhere] + [hbm] * 6 + [smem] * 2,
        [
            pltpu.VMEM(field.shape, F32),
            pltpu.VMEM(cell_scale.shape, F32),
            pltpu.VMEM(cell_scale.shape, I32),
            pltpu.VMEM(size, F32),
            pltpu.VMEM(size, F32),
            pltpu.VMEM((blocks, width), I32),
            dma((6,)),
        ],
        flops=10**11,
        moved=10**7,
    )(returning, *map(in_hbm, (field, cell_scale, material_id, near, far, nodes)), stiff_table, mass_table)
    slots = shape((MOST, 8, width), F32)
    own, twin = call(functools.partial(choose_kernel, tiles), "choose", (slots, slots), [vmem] * 2 + [anywhere])(
        landed.reshape(slab), targets, soil
    )
    twin = lax.ppermute(twin, "tile", pair)
    sums = (6, rows, nz)
    result = pl.pallas_call(
        scatter_kernel,
        out_shape=shape(sums, F32),
        in_specs=[vmem] * 5,
        out_specs=hbm,
        scratch_shapes=[pltpu.VMEM(sums, F32), dma((2,))],
        compiler_params=pltpu.CompilerParams(vmem_limit_bytes=16 * 1024 * 1024),
        cost_estimate=pl.CostEstimate(flops=10**8, bytes_accessed=10**6, transcendentals=0),
        name="scatter",
    )(soil.reshape(sums), own, twin, at_row, at_column)
    return result.reshape(displacement.shape)


def solution(mesh):
    placed = (
        P(None, None, ("freq", "tile"), None, None),
        P("tile", None, None),
        P("tile", None, None),
        P(None, "freq"),
        P(None, "freq"),
        P(("freq", "tile"), None, None, None),
        P("freq"),
        P(),
    )
    return jax.shard_map(
        per_device,
        mesh=mesh,
        in_specs=placed,
        out_specs=P(None, None, ("freq", "tile"), None, None),
        check_vma=False,
    )
```

```python
import functools

import jax
import jax.numpy as jnp
from jax import lax
from jax.experimental import pallas as pl
from jax.experimental.pallas import tpu as pltpu
from jax.sharding import PartitionSpec as P

MOST = 8
F32 = jnp.float32
BF16 = jnp.bfloat16
I32 = jnp.int32
NT = (((1,), (1,)), ((), ()))


def iota(shape, axis):
    return lax.broadcasted_iota(I32, shape, axis)


def onehot(mask):
    return jnp.where(mask, 1.0, 0.0).astype(BF16)


def dot(left, right):
    return jnp.dot(left, right, preferred_element_type=F32)


def dot_nt(left, right):
    return lax.dot_general(left, right, NT, preferred_element_type=F32)


def slots_of(nodes, me, cells, columns):
    blocks, width = nodes.shape
    local = nodes - me * cells
    inside = (local >= 0) & (local < cells)
    shift = columns.bit_length() - 1
    row1 = jnp.where(inside, (local >> shift) + 1, 0).astype(F32).astype(BF16)
    column = jnp.where(inside, local & (columns - 1), 0).astype(F32).astype(BF16)
    first = onehot(iota((MOST, width), 1) == 0)
    onto = dot_nt(first, onehot(inside))
    upper = onehot(iota((blocks, blocks), 0) < iota((blocks, blocks), 1))
    rank = dot(onto.astype(BF16), upper)
    slot = (onto > 0.5) & (rank == iota((MOST, blocks), 0).astype(F32))
    places = dot(onehot(slot), jnp.concatenate([row1, column], axis=1)).astype(I32)
    return slot, places[:, :width] - 1, places[:, width:]


def gather_kernel(
    tiles,
    displacement_hbm,
    nodes_hbm,
    owner_hbm,
    picked_ref,
    displacement,
    node_buffer,
    owner_buffer,
    semaphores,
):
    me = lax.axis_index("tile")
    copies = [
        pltpu.make_async_copy(source, target, semaphores.at[i])
        for i, (source, target) in enumerate(
            ((nodes_hbm, node_buffer), (owner_hbm, owner_buffer), (displacement_hbm, displacement))
        )
    ]
    for copy in copies:
        copy.start()
    copies[0].wait()
    copies[1].wait()
    components, rows, columns = displacement.shape
    blocks, width = node_buffer.shape
    block_count = blocks // tiles
    nodes = node_buffer[...]
    owner = owner_buffer[...]
    cells = rows * columns
    slot, slot_row, slot_column = slots_of(nodes, me, cells, columns)
    target = jnp.concatenate([owner + (b * tiles + 1) for b in range(block_count)], axis=1)
    target = jnp.sum(jnp.where(slot, target.astype(F32), 0.0), axis=1, keepdims=True)
    target = jnp.broadcast_to(target, (MOST, width))
    copies[2].wait()
    field = displacement[...].reshape(components * rows, columns).astype(BF16)
    empty = jnp.zeros((7 - components, width), F32)
    for pair in range(MOST // 2):
        at_column = jnp.concatenate(
            [
                onehot(iota((columns, width), 0) == slot_column[s : s + 1, :])
                for s in (2 * pair, 2 * pair + 1)
            ],
            axis=1,
        )
        taken = dot(field, at_column)
        for i in range(2):
            s = 2 * pair + i
            at_row = iota((rows, width), 0) == slot_row[s : s + 1, :]
            found = []
            for r in range(components):
                k = component(r)
                one = taken[k * rows : (k + 1) * rows, i * width : (i + 1) * width]
                found.append(jnp.sum(jnp.where(at_row, one, 0.0), axis=0, keepdims=True))
            picked_ref[s] = jnp.concatenate(found + [target[s : s + 1, :], empty], axis=0)


def component(row):
    return (row & 1) * 3 + (row >> 1)


def payload_rows(targets, row, tiles, core):
    owner = targets & (tiles - 1)
    block = targets >> (tiles.bit_length() - 1)
    code = (owner >> 1) * 18 + block * 2 + (row >> 1) * 6 + (row & 1)
    return jnp.where((targets >= 0) & ((owner & 1) == core) & (row < 6), code, -1)


def place_kernel(tiles, picked_ref, twin_ref, payload_ref, target_ref):
    core = lax.axis_index("tile") & 1
    rows, width = payload_ref.shape
    picked = jnp.concatenate([picked_ref[...].reshape(MOST * 8, width), twin_ref[...].reshape(MOST * 8, width)], axis=0)
    targets = jnp.concatenate([ref[s, 6:7, :] for ref in (picked_ref, twin_ref) for s in range(MOST)], axis=0)
    targets = targets.astype(I32) - 1
    target_ref[...] = targets
    lane = iota((2 * MOST, width), 1)
    code = payload_rows(targets, lane & 7, tiles, core)
    code = jnp.sum(jnp.where((lane >> 3) == iota((2 * MOST, width), 0), code, 0), axis=0, keepdims=True)
    place = onehot(iota((rows, width), 0) == code)
    payload_ref[...] = dot(place, picked.astype(BF16)).astype(BF16)


def pile_kernel(arrived_ref, imag_ref, more_ref, block_hbm, chip_ref, order_ref, payload_ref, real_ref, semaphores):
    rows, width = payload_ref.shape
    _, pieces, _, _ = arrived_ref.shape
    order = imag_ref.shape[0]
    ahead = more_ref.shape[0]
    ends = (ahead, 640, order)
    copies = []
    for i, (start, stop) in enumerate(zip(ends, ends[1:])):
        copies.append(pltpu.make_async_copy(block_hbm.at[0, start:stop], real_ref.at[start:stop], semaphores.at[i]))
        copies[i].start()
    vector = jnp.sum(arrived_ref[...].astype(F32), axis=0)
    vector = jnp.concatenate([vector[k] for k in range(pieces)], axis=1).astype(BF16)
    by_imag = dot_nt(vector, imag_ref[...])
    by_real = [dot_nt(vector, more_ref[...])]
    for i, (start, stop) in enumerate(zip(ends, ends[1:])):
        copies[i].wait()
        by_real.append(dot_nt(vector, real_ref[start:stop, :]))
    by_real = jnp.concatenate(by_real, axis=1)
    real = by_real[0:1] - by_imag[1:2]
    imag = by_real[1:2] + by_imag[0:1]
    traction = [part[:, k * width : (k + 1) * width] for k in range(pieces) for part in (real, imag)]
    traction = jnp.concatenate(traction + [jnp.zeros((width - 2 * pieces, width), F32)], axis=0).astype(BF16)
    lane = iota((1, width), 1)
    block = (lane >> 1) % 3
    chip = chip_ref[0:1, :]
    for b in (1, 2):
        chip = jnp.where(block == b, chip_ref[b : b + 1, :], chip)
    code = jnp.where(lane < 2 * pieces, chip * (2 * pieces) + lane, -1)
    place = onehot(iota((rows, width), 0) == code)
    payload_ref[...] = dot(place, traction).astype(BF16)


def choose_kernel(landed_ref, take_ref, own_ref):
    own_ref[...] = dot(take_ref[0], landed_ref[...])


def scatter_kernel(soil_ref, own_ref, twin_ref, take_ref, at_row_ref, at_column_ref, result_hbm, result, semaphores):
    components, rows, columns = soil_ref.shape
    pieces = own_ref[...] + dot(take_ref[1], twin_ref[...])
    pieces = jnp.concatenate([pieces[s * 8 : (s + 1) * 8] for s in range(MOST)], axis=1)
    at_row = at_row_ref[...]
    half = components // 2
    copies = []
    for i in range(2):
        spread = []
        for k in range(i * half, (i + 1) * half):
            row = (k % half) * 2 + i
            spread.append(jnp.broadcast_to(pieces[row : row + 1, :], at_row.shape).astype(BF16) * at_row)
        added = dot_nt(jnp.concatenate(spread, axis=0), at_column_ref[...])
        part = slice(i * half, (i + 1) * half)
        result[part] = soil_ref[part] + added.reshape(half, rows, columns)
        copies.append(pltpu.make_async_copy(result.at[part], result_hbm.at[part], semaphores.at[i]))
        copies[i].start()
    for copy in copies:
        copy.wait()


def ahead_kernel(
    order_ref,
    displacement_hbm,
    scale_hbm,
    kind_hbm,
    block_hbm,
    nodes_hbm,
    owner_hbm,
    near_hbm,
    far_hbm,
    imag_ref,
    more_ref,
    chip_ref,
    near,
    far,
    kind,
    node_buffer,
    owner_buffer,
    semaphores,
):
    planes = scale_hbm.shape[0]
    odd = lax.axis_index("tile") & 1
    sides = ((near, near_hbm, (1 - odd) * (planes - 1)), (far, far_hbm, odd * (planes - 1)))
    pairs = [(kind_hbm, kind)]
    for plane, _, x in sides:
        pairs += [(displacement_hbm.at[:, x], plane.at[0:6]), (scale_hbm.at[x], plane.at[6])]
    pairs += [(block_hbm.at[1], imag_ref), (block_hbm.at[0, 0 : more_ref.shape[0]], more_ref)]
    pairs += [(nodes_hbm, node_buffer), (owner_hbm, owner_buffer)]
    copies = [pltpu.make_async_copy(*pair, semaphores.at[i]) for i, pair in enumerate(pairs)]
    for copy in copies:
        copy.start()
    copies[0].wait()
    for plane, _, x in sides:
        plane[7] = kind[x].astype(F32)
    sends = []
    for i, (plane, target, _) in enumerate(sides):
        copies[2 * i + 1].wait()
        copies[2 * i + 2].wait()
        sends.append(pltpu.make_async_copy(plane, target, semaphores.at[9 + i]))
        sends[i].start()
    copies[7].wait()
    copies[8].wait()
    blocks, width = node_buffer.shape
    tiles = owner_buffer.shape[1]
    cells = planes * displacement_hbm.shape[2] * displacement_hbm.shape[3]
    first = onehot(iota((MOST, width), 1) == 0)
    tile_of = jnp.floor(((node_buffer[...] >> 13).astype(F32) + 0.5) * (1.0 / (cells >> 13)))
    tile_row = dot_nt(first, tile_of.astype(BF16))[0:1, :]
    mine = owner_buffer[...] == lax.axis_index("tile")
    for b in range(blocks // tiles):
        own = jnp.sum(jnp.where(mine, tile_row[:, b * tiles : (b + 1) * tiles], 0.0), axis=1, keepdims=True)
        chip_ref[b : b + 1, :] = jnp.broadcast_to(own.astype(I32) >> 1, (1, width))
    for copy in copies[5:7] + sends:
        copy.wait()


def token_kernel(order_ref, token_ref):
    token_ref[...] = jnp.zeros(token_ref.shape, F32)


def lookup(table_ref, row, kind):
    bits = [(kind & (1 << k)) != 0 for k in range(4)]
    level = [table_ref[row, k] for k in range(16)]
    for bit in bits:
        level = [jnp.where(bit, level[2 * k + 1], level[2 * k]) for k in range(len(level) // 2)]
    return level[0]


def half_stiffness(table_ref, kind, scale):
    return [0.5 * (lookup(table_ref, i, kind) * scale) for i in range(2)]


def flux(face, near, far):
    strain = [near[k] - far[k] for k in range(6)]
    real = [face[0] * strain[c] - face[1] * strain[3 + c] for c in range(3)]
    imag = [face[0] * strain[3 + c] + face[1] * strain[c] for c in range(3)]
    return real + imag


def soil_kernel(
    tiles,
    order_ref,
    displacement_hbm,
    scale_hbm,
    kind_hbm,
    near_hbm,
    far_hbm,
    nodes_hbm,
    stiff_ref,
    mass_ref,
    target_ref,
    soil_ref,
    at_row_ref,
    at_column_ref,
    take_ref,
    displacement_ref,
    scale_ref,
    kind_ref,
    near_ref,
    far_ref,
    node_buffer,
    semaphores,
):
    sources = (nodes_hbm, kind_hbm, scale_hbm, displacement_hbm, near_hbm, far_hbm)
    targets = (node_buffer, kind_ref, scale_ref, displacement_ref, near_ref, far_ref)
    copies = [pltpu.make_async_copy(*two, semaphores.at[i]) for i, two in enumerate(zip(sources, targets))]
    for copy in copies:
        copy.start()
    _, planes, ny, nz = displacement_ref.shape
    shape = (ny, nz)
    tile = lax.axis_index("tile")
    odd = tile & 1
    even = odd == 0
    copies[0].wait()
    width = node_buffer.shape[1]
    _, slot_row, slot_column = slots_of(node_buffer[...], tile, planes * ny * nz, nz)
    for s in range(MOST):
        lanes = slice(s * width, (s + 1) * width)
        at_row_ref[:, lanes] = onehot(iota((planes * ny, width), 0) == slot_row[s : s + 1, :])
        at_column_ref[:, lanes] = onehot(iota((nz, width), 0) == slot_column[s : s + 1, :])
    shape3 = (MOST, 8, take_ref.shape[2])
    for i, core in enumerate((odd, 1 - odd)):
        code = payload_rows(target_ref[0:MOST, 0:1].reshape(MOST, 1, 1), iota((MOST, 8, 1), 1), tiles, core)
        take_ref[i] = onehot(iota(shape3, 2) == code).reshape(take_ref.shape[1:])
    for copy in copies[1:]:
        copy.wait()

    @pl.when((tile == 0) | (tile == tiles - 1))
    def _():
        far_ref[...] = jnp.zeros(far_ref.shape, F32)

    at_y, at_z = iota(shape, 0), iota(shape, 1)
    y_last, z_last = at_y == ny - 1, at_z == nz - 1
    edges = (
        jnp.where(at_y == 0, 0.5, 0.0)
        + jnp.where(y_last, 0.5, 0.0)
        + jnp.where(at_z == 0, 0.5, 0.0)
        + jnp.where(z_last, 0.5, 0.0)
    )
    half = [half_stiffness(stiff_ref, kind_ref[x], scale_ref[x]) for x in range(planes)]
    fields = [[displacement_ref[k, x] for k in range(6)] for x in range(planes)]

    def outside(first, second, flag):
        return [jnp.where(flag, first[k], second[k]) for k in range(6)], [
            jnp.where(flag, a, b)
            for a, b in zip(*(half_stiffness(stiff_ref, ref[7].astype(I32), ref[6]) for ref in (first, second)))
        ]

    before, before_half = outside(far_ref, near_ref, even)
    after, after_half = outside(near_ref, far_ref, even)
    fields = [before] + fields + [after]
    half = [before_half] + half + [after_half]

    def x_flux(x):
        return flux([half[x][i] + half[x + 1][i] for i in range(2)], fields[x], fields[x + 1])

    before = x_flux(0)
    for x in range(planes):
        u, own = fields[x + 1], half[x + 1]
        diagonal = [lookup(mass_ref, i, kind_ref[x]) + 2.0 * edges * own[i] for i in range(2)]
        total = [diagonal[0] * u[c] - diagonal[1] * u[3 + c] for c in range(3)]
        total += [diagonal[0] * u[3 + c] + diagonal[1] * u[c] for c in range(3)]
        beyond = x_flux(x + 1)
        total = [total[k] + beyond[k] - before[k] for k in range(6)]
        before = beyond
        for axis, last in ((0, y_last), (1, z_last)):
            size = shape[axis]
            face = [jnp.where(last, 0.0, own[i] + pltpu.roll(own[i], size - 1, axis)) for i in range(2)]
            next_to = [pltpu.roll(u[k], size - 1, axis) for k in range(6)]
            along = flux(face, u, next_to)
            total = [total[k] + along[k] - pltpu.roll(along[k], 1, axis) for k in range(6)]
        for k in range(6):
            soil_ref[k, x] = total[k]


def per_device(
    displacement,
    cell_scale,
    material_id,
    stiff_table,
    mass_table,
    pile_block,
    pile_owner,
    node_index,
):
    planes, ny, nz = cell_scale.shape
    rows = planes * ny
    tiles = lax.axis_size("tile")
    chips = tiles // 2
    _, block_count, width = node_index.shape
    blocks = tiles * block_count
    vmem = pl.BlockSpec(memory_space=pltpu.VMEM)
    smem = pl.BlockSpec(memory_space=pltpu.SMEM)
    hbm = pl.BlockSpec(memory_space=pltpu.HBM)
    anywhere = pl.BlockSpec(memory_space=pl.ANY)
    dma = pltpu.SemaphoreType.DMA

    def call(kernel, name, out_shape, in_specs, scratch=(), flops=10**8, moved=10**6):
        return pl.pallas_call(
            kernel,
            out_shape=out_shape,
            in_specs=in_specs,
            out_specs=jax.tree.map(lambda _: vmem, out_shape),
            scratch_shapes=list(scratch),
            compiler_params=pltpu.CompilerParams(vmem_limit_bytes=16 * 1024 * 1024),
            cost_estimate=pl.CostEstimate(flops=flops, bytes_accessed=moved, transcendentals=0),
            name=name,
        )

    def in_hbm(array):
        return pltpu.with_memory_space_constraint(array, pltpu.HBM)

    def shape(dims, kind):
        return jax.ShapeDtypeStruct(dims, kind)

    field = displacement.reshape(6, planes, ny, nz)
    nodes = node_index.transpose(1, 0, 2).reshape(blocks, width)
    owner = pile_owner.reshape(1, tiles)
    slab = (chips * 18, width)
    cut = (chips, 9, 2, width)
    pair = [(i, i ^ 1) for i in range(tiles)]
    groups = [[2 * chip + core for chip in range(chips)] for core in range(2)]

    size = (8, ny, nz)

    def exchange(payload):
        return lax.all_to_all(payload.reshape(cut), "tile", 0, 0, axis_index_groups=groups, tiled=True)

    picked = call(
        functools.partial(gather_kernel, tiles),
        "gather",
        shape((MOST, 8, width), F32),
        [hbm] * 3,
        [
            pltpu.VMEM((6, rows, nz), F32),
            pltpu.VMEM((blocks, width), I32),
            pltpu.VMEM((1, tiles), I32),
            dma((3,)),
        ],
    )(in_hbm(displacement.reshape(6, rows, nz)), in_hbm(nodes), in_hbm(owner))
    payload, targets = call(
        functools.partial(place_kernel, tiles),
        "place",
        (shape(slab, BF16), shape((2 * MOST, width), I32)),
        [vmem] * 2,
    )(picked, lax.ppermute(picked, "tile", pair))
    arrived = exchange(payload)

    order = pile_block.shape[-1]
    block = in_hbm(pile_block.reshape(2, order, order))
    square = (order, order)
    some = (256, order)
    to_near, to_far, imag, more, chip = pl.pallas_call(
        ahead_kernel,
        out_shape=(shape(size, F32), shape(size, F32), shape(square, BF16), shape(some, BF16), shape((MOST, width), I32)),
        in_specs=[anywhere] + [hbm] * 6,
        out_specs=(hbm, hbm, vmem, vmem, vmem),
        scratch_shapes=[
            pltpu.VMEM(size, F32),
            pltpu.VMEM(size, F32),
            pltpu.VMEM(material_id.shape, I32),
            pltpu.VMEM((blocks, width), I32),
            pltpu.VMEM((1, tiles), I32),
            dma((11,)),
        ],
        compiler_params=pltpu.CompilerParams(vmem_limit_bytes=16 * 1024 * 1024),
        cost_estimate=pl.CostEstimate(flops=10**8, bytes_accessed=10**6, transcendentals=0),
        name="ahead",
    )(payload, *map(in_hbm, (field, cell_scale, material_id)), block, in_hbm(nodes), in_hbm(owner))
    near = lax.ppermute(to_near, "tile", pair)
    next_chip = [(i, (i + 1) % tiles) for i in range(1, tiles, 2)]
    far = lax.ppermute(to_far, "tile", next_chip + [(j, i) for i, j in next_chip])
    token = call(token_kernel, "token", shape((8, width), F32), [anywhere], flops=10**11)(to_far)
    returning = call(
        pile_kernel,
        "pile",
        shape(slab, BF16),
        [vmem, vmem, vmem, hbm, vmem, anywhere],
        [pltpu.VMEM(square, BF16), dma((2,))],
    )(arrived, imag, more, block, chip, token)
    landed = exchange(returning)
    soil, at_row, at_column, take = call(
        functools.partial(soil_kernel, tiles),
        "soil",
        (shape(field.shape, F32), shape((rows, MOST * width), BF16), shape((nz, MOST * width), BF16), shape((2, MOST * 8, chips * 18), BF16)),
        [anywhere] + [hbm] * 6 + [smem] * 2 + [vmem],
        [
            pltpu.VMEM(field.shape, F32),
            pltpu.VMEM(cell_scale.shape, F32),
            pltpu.VMEM(cell_scale.shape, I32),
            pltpu.VMEM(size, F32),
            pltpu.VMEM(size, F32),
            pltpu.VMEM((blocks, width), I32),
            dma((6,)),
        ],
        flops=10**11,
        moved=10**7,
    )(returning, *map(in_hbm, (field, cell_scale, material_id, near, far, nodes)), stiff_table, mass_table, targets)
    landed, soil = lax.optimization_barrier((landed.reshape(slab), soil))
    twin = lax.ppermute(landed, "tile", pair)
    own = call(choose_kernel, "choose", shape((MOST * 8, width), F32), [vmem] * 2, flops=10**11)(landed, take)
    sums = (6, rows, nz)
    result = pl.pallas_call(
        scatter_kernel,
        out_shape=shape(sums, F32),
        in_specs=[vmem] * 6,
        out_specs=hbm,
        scratch_shapes=[pltpu.VMEM(sums, F32), dma((2,))],
        compiler_params=pltpu.CompilerParams(vmem_limit_bytes=16 * 1024 * 1024),
        cost_estimate=pl.CostEstimate(flops=10**8, bytes_accessed=10**6, transcendentals=0),
        name="scatter",
    )(soil.reshape(sums), own, twin, take, at_row, at_column)
    return result.reshape(displacement.shape)


def solution(mesh):
    placed = (
        P(None, None, ("freq", "tile"), None, None),
        P("tile", None, None),
        P("tile", None, None),
        P(None, "freq"),
        P(None, "freq"),
        P(("freq", "tile"), None, None, None),
        P("freq"),
        P(),
    )
    return jax.shard_map(
        per_device,
        mesh=mesh,
        in_specs=placed,
        out_specs=P(None, None, ("freq", "tile"), None, None),
        check_vma=False,
    )
```

```python
import functools

import jax
import jax.numpy as jnp
from jax import lax
from jax.experimental import pallas as pl
from jax.experimental.pallas import tpu as pltpu
from jax.sharding import PartitionSpec as P

MOST = 8
F32 = jnp.float32
BF16 = jnp.bfloat16
I32 = jnp.int32
NT = (((1,), (1,)), ((), ()))


def iota(shape, axis):
    return lax.broadcasted_iota(I32, shape, axis)


def onehot(mask):
    return jnp.where(mask, 1.0, 0.0).astype(BF16)


def dot(left, right):
    return jnp.dot(left, right, preferred_element_type=F32)


def dot_nt(left, right):
    return lax.dot_general(left, right, NT, preferred_element_type=F32)


def slots_of(nodes, me, cells, columns):
    blocks, width = nodes.shape
    local = nodes - me * cells
    inside = (local >= 0) & (local < cells)
    shift = columns.bit_length() - 1
    row1 = jnp.where(inside, (local >> shift) + 1, 0).astype(F32).astype(BF16)
    column = jnp.where(inside, local & (columns - 1), 0).astype(F32).astype(BF16)
    first = onehot(iota((MOST, width), 1) == 0)
    onto = dot_nt(first, onehot(inside))
    upper = onehot(iota((blocks, blocks), 0) < iota((blocks, blocks), 1))
    rank = dot(onto.astype(BF16), upper)
    slot = (onto > 0.5) & (rank == iota((MOST, blocks), 0).astype(F32))
    places = dot(onehot(slot), jnp.concatenate([row1, column], axis=1)).astype(I32)
    return slot, places[:, :width] - 1, places[:, width:]


def gather_kernel(
    tiles,
    displacement_hbm,
    nodes_hbm,
    owner_hbm,
    picked_ref,
    displacement,
    node_buffer,
    owner_buffer,
    semaphores,
):
    me = lax.axis_index("tile")
    copies = [
        pltpu.make_async_copy(source, target, semaphores.at[i])
        for i, (source, target) in enumerate(
            ((nodes_hbm, node_buffer), (owner_hbm, owner_buffer), (displacement_hbm, displacement))
        )
    ]
    for copy in copies:
        copy.start()
    copies[0].wait()
    copies[1].wait()
    components, rows, columns = displacement.shape
    blocks, width = node_buffer.shape
    block_count = blocks // tiles
    nodes = node_buffer[...]
    owner = owner_buffer[...]
    cells = rows * columns
    slot, slot_row, slot_column = slots_of(nodes, me, cells, columns)
    target = jnp.concatenate([owner + (b * tiles + 1) for b in range(block_count)], axis=1)
    target = jnp.sum(jnp.where(slot, target.astype(F32), 0.0), axis=1, keepdims=True)
    target = jnp.broadcast_to(target, (MOST, width))
    copies[2].wait()
    field = displacement[...].reshape(components * rows, columns).astype(BF16)
    empty = jnp.zeros((7 - components, width), F32)
    for pair in range(MOST // 2):
        at_column = jnp.concatenate(
            [
                onehot(iota((columns, width), 0) == slot_column[s : s + 1, :])
                for s in (2 * pair, 2 * pair + 1)
            ],
            axis=1,
        )
        taken = dot(field, at_column)
        for i in range(2):
            s = 2 * pair + i
            at_row = iota((rows, width), 0) == slot_row[s : s + 1, :]
            found = []
            for r in range(components):
                k = component(r)
                one = taken[k * rows : (k + 1) * rows, i * width : (i + 1) * width]
                found.append(jnp.sum(jnp.where(at_row, one, 0.0), axis=0, keepdims=True))
            picked_ref[s] = jnp.concatenate(found + [target[s : s + 1, :], empty], axis=0)


def component(row):
    return (row & 1) * 3 + (row >> 1)


def payload_rows(targets, row, tiles, core):
    owner = targets & (tiles - 1)
    block = targets >> (tiles.bit_length() - 1)
    code = (owner >> 1) * 18 + block * 2 + (row >> 1) * 6 + (row & 1)
    return jnp.where((targets >= 0) & ((owner & 1) == core) & (row < 6), code, -1)


def place_kernel(tiles, picked_ref, twin_ref, payload_ref, target_ref):
    core = lax.axis_index("tile") & 1
    rows, width = payload_ref.shape
    picked = jnp.concatenate([picked_ref[...].reshape(MOST * 8, width), twin_ref[...].reshape(MOST * 8, width)], axis=0)
    targets = jnp.concatenate([ref[s, 6:7, :] for ref in (picked_ref, twin_ref) for s in range(MOST)], axis=0)
    targets = targets.astype(I32) - 1
    target_ref[...] = targets
    lane = iota((2 * MOST, width), 1)
    code = payload_rows(targets, lane & 7, tiles, core)
    code = jnp.sum(jnp.where((lane >> 3) == iota((2 * MOST, width), 0), code, 0), axis=0, keepdims=True)
    place = onehot(iota((rows, width), 0) == code)
    payload_ref[...] = dot(place, picked.astype(BF16)).astype(BF16)


def pile_kernel(arrived_ref, imag_ref, more_ref, block_hbm, chip_ref, order_ref, payload_ref, real_ref, semaphores):
    rows, width = payload_ref.shape
    _, pieces, _, _ = arrived_ref.shape
    order = imag_ref.shape[0]
    ahead = more_ref.shape[0]
    ends = (ahead, 640, order)
    copies = []
    for i, (start, stop) in enumerate(zip(ends, ends[1:])):
        copies.append(pltpu.make_async_copy(block_hbm.at[0, start:stop], real_ref.at[start:stop], semaphores.at[i]))
        copies[i].start()
    lane = iota((1, width), 1)
    block = (lane >> 1) % 3
    chip = chip_ref[0:1, :]
    for b in (1, 2):
        chip = jnp.where(block == b, chip_ref[b : b + 1, :], chip)
    code = jnp.where(lane < 2 * pieces, chip * (2 * pieces) + lane, -1)
    place = onehot(iota((rows, width), 0) == code)
    vector = jnp.sum(arrived_ref[...], axis=0)
    vector = jnp.concatenate([vector[k] for k in range(pieces)], axis=1).astype(BF16)
    by_imag = dot_nt(vector, imag_ref[...])
    by_real = [dot_nt(vector, more_ref[...])]
    for i, (start, stop) in enumerate(zip(ends, ends[1:])):
        copies[i].wait()
        by_real.append(dot_nt(vector, real_ref[start:stop, :]))
    by_real = jnp.concatenate(by_real, axis=1)
    real = by_real[0:1] - by_imag[1:2]
    imag = by_real[1:2] + by_imag[0:1]
    traction = [part[:, k * width : (k + 1) * width] for k in range(pieces) for part in (real, imag)]
    traction = jnp.concatenate(traction + [jnp.zeros((width - 2 * pieces, width), F32)], axis=0).astype(BF16)
    payload_ref[...] = dot(place, traction).astype(BF16)


def choose_kernel(landed_ref, take_ref, own_ref):
    own_ref[...] = dot(take_ref[0], landed_ref[...])


def scatter_kernel(soil_ref, own_ref, twin_ref, take_ref, at_row_ref, at_column_ref, result_hbm, result, semaphores):
    components, rows, columns = soil_ref.shape
    pieces = own_ref[...] + dot(take_ref[1], twin_ref[...])
    pieces = jnp.concatenate([pieces[s * 8 : (s + 1) * 8] for s in range(MOST)], axis=1)
    at_row = at_row_ref[...]
    half = components // 2
    copies = []
    for i, (start, stop) in enumerate(((0, 4), (4, components))):
        spread = []
        for k in range(start, stop):
            row = (k % half) * 2 + k // half
            spread.append(jnp.broadcast_to(pieces[row : row + 1, :], at_row.shape).astype(BF16) * at_row)
        added = dot_nt(jnp.concatenate(spread, axis=0), at_column_ref[...])
        result[start:stop] = soil_ref[start:stop] + added.reshape(stop - start, rows, columns)
        copies.append(pltpu.make_async_copy(result.at[start:stop], result_hbm.at[start:stop], semaphores.at[i]))
        copies[i].start()
    for copy in copies:
        copy.wait()


def ahead_kernel(
    order_ref,
    displacement_hbm,
    scale_hbm,
    kind_hbm,
    block_hbm,
    nodes_hbm,
    owner_hbm,
    near_hbm,
    far_hbm,
    imag_ref,
    more_ref,
    chip_ref,
    near,
    far,
    kind,
    node_buffer,
    owner_buffer,
    semaphores,
):
    planes = scale_hbm.shape[0]
    odd = lax.axis_index("tile") & 1
    sides = ((near, near_hbm, (1 - odd) * (planes - 1)), (far, far_hbm, odd * (planes - 1)))
    pairs = [(kind_hbm, kind)]
    for plane, _, x in sides:
        pairs += [(displacement_hbm.at[:, x], plane.at[0:6]), (scale_hbm.at[x], plane.at[6])]
    pairs += [(block_hbm.at[1], imag_ref), (block_hbm.at[0, 0 : more_ref.shape[0]], more_ref)]
    pairs += [(nodes_hbm, node_buffer), (owner_hbm, owner_buffer)]
    copies = [pltpu.make_async_copy(*pair, semaphores.at[i]) for i, pair in enumerate(pairs)]
    for copy in copies:
        copy.start()
    copies[0].wait()
    for plane, _, x in sides:
        plane[7] = kind[x].astype(F32)
    sends = []
    for i, (plane, target, _) in enumerate(sides):
        copies[2 * i + 1].wait()
        copies[2 * i + 2].wait()
        sends.append(pltpu.make_async_copy(plane, target, semaphores.at[9 + i]))
        sends[i].start()
    copies[7].wait()
    copies[8].wait()
    blocks, width = node_buffer.shape
    tiles = owner_buffer.shape[1]
    cells = planes * displacement_hbm.shape[2] * displacement_hbm.shape[3]
    first = onehot(iota((MOST, width), 1) == 0)
    tile_of = jnp.floor(((node_buffer[...] >> 13).astype(F32) + 0.5) * (1.0 / (cells >> 13)))
    tile_row = dot_nt(first, tile_of.astype(BF16))[0:1, :]
    mine = owner_buffer[...] == lax.axis_index("tile")
    for b in range(blocks // tiles):
        own = jnp.sum(jnp.where(mine, tile_row[:, b * tiles : (b + 1) * tiles], 0.0), axis=1, keepdims=True)
        chip_ref[b : b + 1, :] = jnp.broadcast_to(own.astype(I32) >> 1, (1, width))
    for copy in copies[5:7] + sends:
        copy.wait()


def token_kernel(order_ref, token_ref):
    token_ref[...] = jnp.zeros(token_ref.shape, F32)


def lookup(table_ref, row, kind):
    bits = [(kind & (1 << k)) != 0 for k in range(4)]
    level = [table_ref[row, k] for k in range(16)]
    for bit in bits:
        level = [jnp.where(bit, level[2 * k + 1], level[2 * k]) for k in range(len(level) // 2)]
    return level[0]


def half_stiffness(table_ref, kind, scale):
    return [0.5 * (lookup(table_ref, i, kind) * scale) for i in range(2)]


def flux(face, near, far):
    strain = [near[k] - far[k] for k in range(6)]
    real = [face[0] * strain[c] - face[1] * strain[3 + c] for c in range(3)]
    imag = [face[0] * strain[3 + c] + face[1] * strain[c] for c in range(3)]
    return real + imag


def soil_kernel(
    tiles,
    order_ref,
    displacement_hbm,
    scale_hbm,
    kind_hbm,
    near_hbm,
    far_hbm,
    nodes_hbm,
    stiff_ref,
    mass_ref,
    target_ref,
    soil_ref,
    at_row_ref,
    at_column_ref,
    take_ref,
    displacement_ref,
    scale_ref,
    kind_ref,
    near_ref,
    far_ref,
    node_buffer,
    semaphores,
):
    sources = (nodes_hbm, kind_hbm, scale_hbm, displacement_hbm, near_hbm, far_hbm)
    targets = (node_buffer, kind_ref, scale_ref, displacement_ref, near_ref, far_ref)
    copies = [pltpu.make_async_copy(*two, semaphores.at[i]) for i, two in enumerate(zip(sources, targets))]
    for copy in copies:
        copy.start()
    _, planes, ny, nz = displacement_ref.shape
    shape = (ny, nz)
    tile = lax.axis_index("tile")
    odd = tile & 1
    even = odd == 0
    copies[0].wait()
    width = node_buffer.shape[1]
    _, slot_row, slot_column = slots_of(node_buffer[...], tile, planes * ny * nz, nz)
    for s in range(MOST):
        lanes = slice(s * width, (s + 1) * width)
        at_row_ref[:, lanes] = onehot(iota((planes * ny, width), 0) == slot_row[s : s + 1, :])
        at_column_ref[:, lanes] = onehot(iota((nz, width), 0) == slot_column[s : s + 1, :])
    shape3 = (MOST, 8, take_ref.shape[2])
    for i, core in enumerate((odd, 1 - odd)):
        code = payload_rows(target_ref[0:MOST, 0:1].reshape(MOST, 1, 1), iota((MOST, 8, 1), 1), tiles, core)
        take_ref[i] = onehot(iota(shape3, 2) == code).reshape(take_ref.shape[1:])
    for copy in copies[1:]:
        copy.wait()

    @pl.when((tile == 0) | (tile == tiles - 1))
    def _():
        far_ref[...] = jnp.zeros(far_ref.shape, F32)

    at_y, at_z = iota(shape, 0), iota(shape, 1)
    y_last, z_last = at_y == ny - 1, at_z == nz - 1
    edges = (
        jnp.where(at_y == 0, 0.5, 0.0)
        + jnp.where(y_last, 0.5, 0.0)
        + jnp.where(at_z == 0, 0.5, 0.0)
        + jnp.where(z_last, 0.5, 0.0)
    )
    half = [half_stiffness(stiff_ref, kind_ref[x], scale_ref[x]) for x in range(planes)]
    fields = [[displacement_ref[k, x] for k in range(6)] for x in range(planes)]

    def outside(first, second, flag):
        return [jnp.where(flag, first[k], second[k]) for k in range(6)], [
            jnp.where(flag, a, b)
            for a, b in zip(*(half_stiffness(stiff_ref, ref[7].astype(I32), ref[6]) for ref in (first, second)))
        ]

    before, before_half = outside(far_ref, near_ref, even)
    after, after_half = outside(near_ref, far_ref, even)
    fields = [before] + fields + [after]
    half = [before_half] + half + [after_half]

    def x_flux(x):
        return flux([half[x][i] + half[x + 1][i] for i in range(2)], fields[x], fields[x + 1])

    before = x_flux(0)
    for x in range(planes):
        u, own = fields[x + 1], half[x + 1]
        diagonal = [lookup(mass_ref, i, kind_ref[x]) + 2.0 * edges * own[i] for i in range(2)]
        total = [diagonal[0] * u[c] - diagonal[1] * u[3 + c] for c in range(3)]
        total += [diagonal[0] * u[3 + c] + diagonal[1] * u[c] for c in range(3)]
        beyond = x_flux(x + 1)
        total = [total[k] + beyond[k] - before[k] for k in range(6)]
        before = beyond
        for axis, last in ((0, y_last), (1, z_last)):
            size = shape[axis]
            face = [jnp.where(last, 0.0, own[i] + pltpu.roll(own[i], size - 1, axis)) for i in range(2)]
            next_to = [pltpu.roll(u[k], size - 1, axis) for k in range(6)]
            along = flux(face, u, next_to)
            total = [total[k] + along[k] - pltpu.roll(along[k], 1, axis) for k in range(6)]
        for k in range(6):
            soil_ref[k, x] = total[k]


def per_device(
    displacement,
    cell_scale,
    material_id,
    stiff_table,
    mass_table,
    pile_block,
    pile_owner,
    node_index,
):
    planes, ny, nz = cell_scale.shape
    rows = planes * ny
    tiles = lax.axis_size("tile")
    chips = tiles // 2
    _, block_count, width = node_index.shape
    blocks = tiles * block_count
    vmem = pl.BlockSpec(memory_space=pltpu.VMEM)
    smem = pl.BlockSpec(memory_space=pltpu.SMEM)
    hbm = pl.BlockSpec(memory_space=pltpu.HBM)
    anywhere = pl.BlockSpec(memory_space=pl.ANY)
    dma = pltpu.SemaphoreType.DMA

    def call(kernel, name, out_shape, in_specs, scratch=(), flops=10**8, moved=10**6):
        return pl.pallas_call(
            kernel,
            out_shape=out_shape,
            in_specs=in_specs,
            out_specs=jax.tree.map(lambda _: vmem, out_shape),
            scratch_shapes=list(scratch),
            compiler_params=pltpu.CompilerParams(vmem_limit_bytes=16 * 1024 * 1024),
            cost_estimate=pl.CostEstimate(flops=flops, bytes_accessed=moved, transcendentals=0),
            name=name,
        )

    def in_hbm(array):
        return pltpu.with_memory_space_constraint(array, pltpu.HBM)

    def shape(dims, kind):
        return jax.ShapeDtypeStruct(dims, kind)

    field = displacement.reshape(6, planes, ny, nz)
    nodes = node_index.transpose(1, 0, 2).reshape(blocks, width)
    owner = pile_owner.reshape(1, tiles)
    slab = (chips * 18, width)
    cut = (chips, 9, 2, width)
    pair = [(i, i ^ 1) for i in range(tiles)]
    groups = [[2 * chip + core for chip in range(chips)] for core in range(2)]

    size = (8, ny, nz)

    def exchange(payload):
        return lax.all_to_all(payload.reshape(cut), "tile", 0, 0, axis_index_groups=groups, tiled=True)

    picked = call(
        functools.partial(gather_kernel, tiles),
        "gather",
        shape((MOST, 8, width), F32),
        [hbm] * 3,
        [
            pltpu.VMEM((6, rows, nz), F32),
            pltpu.VMEM((blocks, width), I32),
            pltpu.VMEM((1, tiles), I32),
            dma((3,)),
        ],
    )(in_hbm(displacement.reshape(6, rows, nz)), in_hbm(nodes), in_hbm(owner))
    payload, targets = call(
        functools.partial(place_kernel, tiles),
        "place",
        (shape(slab, BF16), shape((2 * MOST, width), I32)),
        [vmem] * 2,
    )(picked, lax.ppermute(picked, "tile", pair))
    arrived = exchange(payload)

    order = pile_block.shape[-1]
    block = in_hbm(pile_block.reshape(2, order, order))
    square = (order, order)
    some = (256, order)
    to_near, to_far, imag, more, chip = pl.pallas_call(
        ahead_kernel,
        out_shape=(shape(size, F32), shape(size, F32), shape(square, BF16), shape(some, BF16), shape((MOST, width), I32)),
        in_specs=[anywhere] + [hbm] * 6,
        out_specs=(hbm, hbm, vmem, vmem, vmem),
        scratch_shapes=[
            pltpu.VMEM(size, F32),
            pltpu.VMEM(size, F32),
            pltpu.VMEM(material_id.shape, I32),
            pltpu.VMEM((blocks, width), I32),
            pltpu.VMEM((1, tiles), I32),
            dma((11,)),
        ],
        compiler_params=pltpu.CompilerParams(vmem_limit_bytes=16 * 1024 * 1024),
        cost_estimate=pl.CostEstimate(flops=10**8, bytes_accessed=10**6, transcendentals=0),
        name="ahead",
    )(payload, *map(in_hbm, (field, cell_scale, material_id)), block, in_hbm(nodes), in_hbm(owner))
    near = lax.ppermute(to_near, "tile", pair)
    next_chip = [(i, (i + 1) % tiles) for i in range(1, tiles, 2)]
    far = lax.ppermute(to_far, "tile", next_chip + [(j, i) for i, j in next_chip])
    token = call(token_kernel, "token", shape((8, width), F32), [anywhere], flops=10**11)(to_far)
    returning = call(
        pile_kernel,
        "pile",
        shape(slab, BF16),
        [vmem, vmem, vmem, hbm, vmem, anywhere],
        [pltpu.VMEM(square, BF16), dma((2,))],
    )(arrived, imag, more, block, chip, token)
    landed = exchange(returning)
    soil, at_row, at_column, take = call(
        functools.partial(soil_kernel, tiles),
        "soil",
        (shape(field.shape, F32), shape((rows, MOST * width), BF16), shape((nz, MOST * width), BF16), shape((2, MOST * 8, chips * 18), BF16)),
        [anywhere] + [hbm] * 6 + [smem] * 2 + [vmem],
        [
            pltpu.VMEM(field.shape, F32),
            pltpu.VMEM(cell_scale.shape, F32),
            pltpu.VMEM(cell_scale.shape, I32),
            pltpu.VMEM(size, F32),
            pltpu.VMEM(size, F32),
            pltpu.VMEM((blocks, width), I32),
            dma((6,)),
        ],
        flops=10**11,
        moved=10**7,
    )(returning, *map(in_hbm, (field, cell_scale, material_id, near, far, nodes)), stiff_table, mass_table, targets)
    landed, soil = lax.optimization_barrier((landed.reshape(slab), soil))
    twin = lax.ppermute(landed, "tile", pair)
    own = call(choose_kernel, "choose", shape((MOST * 8, width), F32), [vmem] * 2, flops=10**11)(landed, take)
    sums = (6, rows, nz)
    result = pl.pallas_call(
        scatter_kernel,
        out_shape=shape(sums, F32),
        in_specs=[vmem] * 6,
        out_specs=hbm,
        scratch_shapes=[pltpu.VMEM(sums, F32), dma((2,))],
        compiler_params=pltpu.CompilerParams(vmem_limit_bytes=16 * 1024 * 1024),
        cost_estimate=pl.CostEstimate(flops=10**8, bytes_accessed=10**6, transcendentals=0),
        name="scatter",
    )(soil.reshape(sums), own, twin, take, at_row, at_column)
    return result.reshape(displacement.shape)


def solution(mesh):
    placed = (
        P(None, None, ("freq", "tile"), None, None),
        P("tile", None, None),
        P("tile", None, None),
        P(None, "freq"),
        P(None, "freq"),
        P(("freq", "tile"), None, None, None),
        P("freq"),
        P(),
    )
    return jax.shard_map(
        per_device,
        mesh=mesh,
        in_specs=placed,
        out_specs=P(None, None, ("freq", "tile"), None, None),
        check_vma=False,
    )
```
